32 devices in a mesh: ctx: 4 (over y, x), fsdp: 8 (over z, core).
Axes of the slice: x: 2, y: 2, z: 4, core: 2. Of those that a mesh axis runs over, the one named last changes fastest.
Arguments:
- inputs: bfloat16 [8, 1024, 2304], P('fsdp', 'ctx'), may hold values from -5 to 5
- positions: int32 [8, 1024], P('fsdp', 'ctx'), may hold values from 0 to 1023, as said below
- pre_attn_gain: bfloat16 [2304], P('fsdp'), may hold values from 0.099609375 to 1.8984375
- post_attn_gain: bfloat16 [2304], P('fsdp'), may hold values from 0.099609375 to 1.8984375
- pre_mlp_gain: bfloat16 [2304], P('fsdp'), may hold values from 0.099609375 to 1.8984375
- post_mlp_gain: bfloat16 [2304], P('fsdp'), may hold values from 0.099609375 to 1.8984375
- query_weight: bfloat16 [2304, 2048], P('fsdp'), may hold values from -1 to 1
- key_weight: bfloat16 [2304, 1024], P('fsdp'), may hold values from -1 to 1
- value_weight: bfloat16 [2304, 1024], P('fsdp'), may hold values from -0.125 to 0.125
- out_weight: bfloat16 [2048, 2304], P('fsdp'), may hold values from -0.125 to 0.125
- gate_weight: bfloat16 [2304, 9216], P('fsdp'), may hold values from -0.125 to 0.125
- up_weight: bfloat16 [2304, 9216], P('fsdp'), may hold values from -0.125 to 0.125
- down_weight: bfloat16 [9216, 2304], P('fsdp'), may hold values from -0.0625 to 0.0625
- cotangent: bfloat16 [8, 1024, 2304], P('fsdp', 'ctx'), may hold values from -6 to 6
Outputs:
- output: bfloat16 [8, 1024, 2304], P('fsdp', 'ctx')
- input_grad: bfloat16 [8, 1024, 2304], P('fsdp', 'ctx')
- pre_attn_gain_grad: float32 [2304], P('fsdp')
- post_attn_gain_grad: float32 [2304], P('fsdp')
- pre_mlp_gain_grad: float32 [2304], P('fsdp')
- post_mlp_gain_grad: float32 [2304], P('fsdp')
- query_weight_grad: float32 [2304, 2048], P('fsdp')
- key_weight_grad: float32 [2304, 1024], P('fsdp')
- value_weight_grad: float32 [2304, 1024], P('fsdp')
- out_weight_grad: float32 [2048, 2304], P('fsdp')
- gate_weight_grad: float32 [2304, 9216], P('fsdp')
- up_weight_grad: float32 [2304, 9216], P('fsdp')
- down_weight_grad: float32 [9216, 2304], P('fsdp')
The draws below stay inside these ranges and needn't reach their ends.
Inputs may be any that keep to these rules, and one draw needn't show every extreme that they name: Each row is a permutation of the positions of one sequence. The 256 tokens held by one index c of ctx are two runs of 128 consecutive positions, blocks b and 2 n - 1 - b of the sequence (n the number of ctx indices), with b a permutation of the ctx indices drawn for each sequence.
All inputs are finite; a program needn't handle non-finite values.
Results may differ from the reference program's by a relative error of at most 0.029.
Values may be sent and summed in bfloat16 or wider, within the bound.
No kernel may reach another device: no remote copies, remote signals or barrier semaphores. Data moves between devices by JAX's collectives and lax.ppermute only.
A program may use at most 576 MiB of HBM per device.

```python
import jax
import jax.numpy as jnp
from jax import lax

D = 2304
HQ = 8
KV = 4
HD = 256
FF = 9216
SEQ_LEN = 1024
SEQS = 8
SPAN = 128
N_CTX = 4


aligned_scale = 6.4


def shared_signs(key):
    return jnp.where(jax.random.bernoulli(key, 0.5, (D,)), 1.0, -1.0).astype(jnp.float32)


def leading_columns(count):
    column = jnp.arange(count, dtype=jnp.int32) % HD
    half = HD // 2
    pairs = min(16, HD // 4)
    return (column % half >= half - pairs).astype(jnp.float32)


def drawn_weight(key, signs, columns):
    base = jnp.clip(jax.random.normal(key, (D, columns), jnp.float32), -5.0, 5.0) * D ** (-0.5)
    extra = leading_columns(columns)[None, :] * signs[:, None] * (aligned_scale / D)
    return (base + extra).astype(jnp.bfloat16)


def draw_inputs(key, part):
    signs = shared_signs(key)
    key = jax.random.fold_in(key, 21)
    noise = jnp.clip(jax.random.normal(key, (SEQS, SEQ_LEN, D), jnp.float32), -4.0, 4.0)
    return (noise + signs).astype(jnp.bfloat16)


def draw_query_weight(key, part):
    signs = shared_signs(key)
    key = jax.random.fold_in(key, 22)
    return drawn_weight(key, signs, HQ * HD)


def draw_key_weight(key, part):
    signs = shared_signs(key)
    key = jax.random.fold_in(key, 23)
    return drawn_weight(key, signs, KV * HD)


def draw_positions(key, part):
    key = jax.random.fold_in(key, 11)
    subkeys = jax.random.split(key, SEQS)
    orders = jax.vmap(lambda sub: jax.random.permutation(sub, N_CTX))(subkeys)
    offsets = jnp.arange(SPAN, dtype=jnp.int32)
    first = orders[:, :, None] * SPAN + offsets
    second = (2 * N_CTX - 1 - orders)[:, :, None] * SPAN + offsets
    return jnp.concatenate([first, second], axis=2).reshape(SEQS, SEQ_LEN).astype(jnp.int32)


def block_scale(rng, dims, shards, least, high):
    loudness, own = 1.0, jax.random.fold_in(rng, 6)
    for dim, blocks in shards:
        draws = jnp.exp(jax.random.uniform(jax.random.fold_in(own, dim), (blocks,), jnp.float32, least / len(shards), high / len(shards)))
        loudness = loudness * jnp.repeat(draws, dims[dim] // blocks).reshape([-1 if axis == dim else 1 for axis in range(len(dims))])
    return loudness


def scatter_about(stream_key, shape, deviation, most, cuts=(), kind=jnp.bfloat16):
    values = deviation * jax.random.normal(stream_key, shape, jnp.float32)
    if cuts:
        values = values * block_scale(stream_key, shape, cuts, -0.22, 0.18)
    return jnp.clip(values, -most, most).astype(kind)


def setup_inputs(seed: int = 0) -> dict:
    seeds = jax.random.split(jax.random.key(seed), 15)
    return {
        "inputs": draw_inputs(jax.random.fold_in(seeds[14], 71), 0),
        "positions": draw_positions(jax.random.fold_in(seeds[14], 71), 0),
        "pre_attn_gain": jnp.clip(1.0 + 0.18 * jax.random.normal(seeds[2], (D,), jnp.float32), 0.099609375, 1.8984375).astype(jnp.bfloat16),
        "post_attn_gain": jnp.clip(1.0 + 0.18 * jax.random.normal(seeds[3], (D,), jnp.float32), 0.099609375, 1.8984375).astype(jnp.bfloat16),
        "pre_mlp_gain": jnp.clip(1.0 + 0.18 * jax.random.normal(seeds[4], (D,), jnp.float32), 0.099609375, 1.8984375).astype(jnp.bfloat16),
        "post_mlp_gain": jnp.clip(1.0 + 0.18 * jax.random.normal(seeds[5], (D,), jnp.float32), 0.099609375, 1.8984375).astype(jnp.bfloat16),
        "query_weight": draw_query_weight(jax.random.fold_in(seeds[14], 71), 0),
        "key_weight": draw_key_weight(jax.random.fold_in(seeds[14], 71), 0),
        "value_weight": scatter_about(seeds[8], (D, KV * HD), D ** -0.5, 0.125, ((0, 8),)),
        "out_weight": scatter_about(seeds[9], (HQ * HD, D), (HQ * HD) ** -0.5, 0.125, ((0, 8),)),
        "gate_weight": scatter_about(seeds[10], (D, FF), D ** -0.5, 0.125, ((0, 8),)),
        "up_weight": scatter_about(seeds[11], (D, FF), D ** -0.5, 0.125, ((0, 8),)),
        "down_weight": scatter_about(seeds[12], (FF, D), FF ** -0.5, 0.0625, ((0, 8),)),
        "cotangent": scatter_about(seeds[13], (SEQS, SEQ_LEN, D), 1.0, 6.0, ((0, 8), (1, 4))),
    }


@jax.custom_vjp
def low(v):
    return lax.optimization_barrier(v.astype(jnp.bfloat16)).astype(jnp.float32)

@jax.custom_vjp
def low_back(v):
    return v

def low_keep(v):
    return (low(v), None)

def low_pass(kept, grad):
    return (grad,)

def back_keep(v):
    return (v, None)

def back_low(kept, grad):
    return (low(grad),)
low.defvjp(low_keep, low_pass)
low_back.defvjp(back_keep, back_low)
soft_cap = 50.0
epsilon = 1e-06
rope_base = 10000.0
masked_fill = -1e+30

def matmul(left, right):
    return jnp.dot(left, right, precision=lax.Precision.HIGHEST, preferred_element_type=jnp.float32)

def frequencies(half, head_dim):
    return rope_base ** (-(jnp.arange(half, dtype=jnp.float32) * 2.0) / head_dim)

def rotate(vectors, angles):
    half = vectors.shape[-1] // 2
    first = vectors[..., :half]
    second = vectors[..., half:]
    cosine = jnp.cos(angles)[..., None, :]
    sine = jnp.sin(angles)[..., None, :]
    return jnp.concatenate([first * cosine - second * sine, second * cosine + first * sine], axis=-1)

def rms_norm(vectors, gain):
    return vectors * lax.rsqrt(lax.optimization_barrier(jnp.mean(vectors * vectors, axis=-1, keepdims=True)) + epsilon) * gain

def attend(queries, keys, values, places):
    group = queries.shape[1] // keys.shape[1]
    keys = jnp.repeat(keys, group, axis=1)
    values = jnp.repeat(values, group, axis=1)
    raw = low_back(jnp.einsum('qhd,khd->hqk', queries, keys, precision=lax.Precision.HIGHEST))
    capped = soft_cap * jnp.tanh(raw / soft_cap)
    allowed = places[None, :] <= places[:, None]
    capped = jnp.where(allowed[None], capped, masked_fill)
    shifted = capped - lax.optimization_barrier(jnp.max(capped, axis=-1, keepdims=True))
    weights = jnp.exp(shifted)
    weights = weights / lax.optimization_barrier(jnp.sum(weights, axis=-1, keepdims=True))
    return jnp.einsum('hqk,khd->qhd', weights, values, precision=lax.Precision.HIGHEST)

def layer_one(rows, places, params):
    gain_a, gain_b, gain_c, gain_d, w_query, w_key, w_value, w_out, w_gate, w_up, w_down = params
    length = rows.shape[0]
    angles = places.astype(jnp.float32)[:, None] * frequencies(HD // 2, HD)
    normed = low(rms_norm(rows, gain_a))
    query_lin = low_back(matmul(normed, w_query)).reshape(length, HQ, HD)
    key_lin = low_back(matmul(normed, w_key)).reshape(length, KV, HD)
    values = low_back(low(matmul(normed, w_value))).reshape(length, KV, HD)
    queries = low(rotate(query_lin, angles) * HD ** (-0.5))
    keys = low(rotate(key_lin, angles))
    mixed = attend(queries, keys, values, places)
    attn = low_back(low(mixed)).reshape(length, HQ * HD)
    branch = low_back(matmul(attn, w_out))
    middle = rows + rms_norm(branch, gain_b)
    normed_mlp = low(rms_norm(middle, gain_c))
    gate = low_back(matmul(normed_mlp, w_gate))
    up = low_back(matmul(normed_mlp, w_up))
    hidden = low(jax.nn.gelu(gate, approximate=True) * up)
    down = low_back(matmul(hidden, w_down))
    return middle + rms_norm(down, gain_d)

def reference(inputs, positions, pre_attn_gain, post_attn_gain, pre_mlp_gain, post_mlp_gain, query_weight, key_weight, value_weight, out_weight, gate_weight, up_weight, down_weight, cotangent):
    floats = [inputs, pre_attn_gain, post_attn_gain, pre_mlp_gain, post_mlp_gain, query_weight, key_weight, value_weight, out_weight, gate_weight, up_weight, down_weight]
    floats = [item.astype(jnp.float32) for item in floats]

    def whole(rows_all, *params):

        def one_sequence(parts):
            return layer_one(parts[0], parts[1], params)
        return lax.map(jax.checkpoint(one_sequence), (rows_all, positions))
    result, pullback = jax.vjp(whole, *floats)
    grads = pullback(cotangent.astype(jnp.float32))
    return (result.astype(jnp.bfloat16), grads[0].astype(jnp.bfloat16), grads[1], grads[2], grads[3], grads[4], grads[5], grads[6], grads[7], grads[8], grads[9], grads[10], grads[11])
```

```python
import functools

import jax
import jax.numpy as jnp
from jax import lax
from jax.experimental import pallas as pl
from jax.experimental.pallas import tpu as pltpu
from jax.sharding import PartitionSpec as P

HQ = 8
KV = 4
HD = 256

soft_cap = 50.0
epsilon = 1e-06
rope_base = 10000.0
low = jnp.bfloat16
wide = jnp.float32


def swap(shard, axis, mask):
    size = lax.axis_size(axis)
    return lax.ppermute(shard, axis, [(i, i ^ mask) for i in range(size)])


def after(value, *others):
    return lax.optimization_barrier((value, *others))[0]


def chip_groups():
    size = lax.axis_size("fsdp")
    return [list(range(core, size, 2)) for core in (0, 1)]


def cut_at(width):
    return (width // 512) * 256 if width >= 512 else width // 2


def gather_pieces(block, halves=True):
    width = block.shape[-1]
    got, pieces = {0: block}, [(block, 0, 0)]
    for k in range(1, lax.axis_size("ctx")):
        low_bit, high_bit = k & -k, 1 << (k.bit_length() - 1)
        if low_bit == high_bit or not halves:
            got[k] = swap(got[k ^ high_bit], "ctx", high_bit)
            pieces.append((got[k], k, 0))
        else:
            cut = cut_at(width)
            first = swap(got[k ^ high_bit][..., :cut], "ctx", high_bit)
            second = swap(got[k ^ low_bit][..., cut:], "ctx", low_bit)
            pieces += [(first, k, 0), (second, k, cut)]
            if k + 1 < lax.axis_size("ctx"):
                got[k] = jnp.concatenate([first, second], axis=-1)
    return pieces


def gather_blocks(block, halves=True):
    return as_blocks(gather_pieces(block, halves))


def as_blocks(pieces):
    blocks = [[] for _ in range(lax.axis_size("ctx"))]
    for array, k, _ in pieces:
        blocks[k].append(array)
    return [b[0] if len(b) == 1 else jnp.concatenate(b, axis=-1) for b in blocks]


def halved(parts):
    cut = cut_at(parts[0].shape[-1])
    return [(part[..., :cut], part[..., cut:]) for part in parts]


def scatter_sum(terms):
    terms = list(terms)
    for k in range(len(terms) - 1, 0, -1):
        low_bit, high_bit = k & -k, 1 << (k.bit_length() - 1)
        first = swap(terms[k][0], "ctx", high_bit).astype(wide)
        second = swap(terms[k][1], "ctx", low_bit).astype(wide)
        to_first, to_second = k ^ high_bit, k ^ low_bit
        first = terms[to_first][0].astype(wide) + first
        terms[to_first] = (first.astype(low) if to_first else first, terms[to_first][1])
        second = terms[to_second][1].astype(wide) + second
        terms[to_second] = (terms[to_second][0], second.astype(low) if to_second else second)
    return jnp.concatenate(terms[0], axis=-1)


def exchange(parts):
    return [parts[0]] + [swap(part, "ctx", k) for k, part in enumerate(parts) if k]


def chip_sum(term):
    count = lax.axis_size("fsdp")
    core = lax.axis_index("fsdp") & 1
    halves = term.reshape(count // 2, 2, term.shape[0] // count, term.shape[1])
    theirs = swap(lax.dynamic_index_in_dim(halves, 1 - core, 1, keepdims=False), "fsdp", 1)
    mine = lax.dynamic_index_in_dim(halves, core, 1, keepdims=False)
    total = (mine.astype(wide) + theirs.astype(wide)).astype(low)
    return total.reshape(-1, term.shape[1])


def fsdp_sum(arr):
    return lax.psum_scatter(
        arr,
        "fsdp",
        scatter_dimension=0,
        tiled=True,
        axis_index_groups=chip_groups(),
    )


def row_tile(rows):
    return next(t for t in (48, 32, 16, rows) if rows % t == 0)


def unit_place(block, count, main, rest):
    return block % 2 * (count // 2) * (main + rest) + block // 2 * main


def rest_place(core, count, main, rest):
    return core * (count // 2) * (main + rest) + count // 2 * main


def take_units_kernel(count, cols, main, rest, c_ref, weight_ref, pick_ref, out_ref):
    c = c_ref[0]
    for b in range(count):
        start = pl.multiple_of(b * cols + c * main, 128)
        to = unit_place(b, count, main, rest)
        out_ref[:, to : to + main] = weight_ref[:, pl.ds(start, main)]
    last = jnp.concatenate(
        [weight_ref[:, (b + 1) * cols - 128 : (b + 1) * cols] for b in range(count)], axis=1
    )
    picked = jnp.dot(last, pick_ref[...], preferred_element_type=jnp.float32)
    size = count // 2 * rest
    for core in (0, 1):
        to = rest_place(core, count, main, rest)
        out_ref[:, to : to + size] = picked[:, core * size : (core + 1) * size].astype(out_ref.dtype)


def take_units(weight, c, count, main, rest):
    rows, cols = weight.shape
    source = jnp.arange(count * 128)[:, None]
    target = jnp.arange(count * rest)[None, :]
    block = target // rest % (count // 2) * 2 + target // (count // 2 * rest)
    pick = (source == block * 128 + c * rest + target % rest).astype(weight.dtype)
    tile = row_tile(rows)
    return pl.pallas_call(
        functools.partial(take_units_kernel, count, cols // count, main, rest),
        out_shape=jax.ShapeDtypeStruct((rows, count * (main + rest)), weight.dtype),
        grid=(rows // tile,),
        in_specs=[
            pl.BlockSpec(memory_space=pltpu.SMEM),
            pl.BlockSpec((tile, cols), lambda i: (i, 0)),
            pl.BlockSpec(pick.shape, lambda i: (0, 0)),
        ],
        out_specs=pl.BlockSpec((tile, count * (main + rest)), lambda i: (i, 0)),
        compiler_params=pltpu.CompilerParams(vmem_limit_bytes=32 * 2**20),
        cost_estimate=pl.CostEstimate(
            flops=2 * rows * count * 128 * count * rest,
            bytes_accessed=3 * rows * cols,
            transcendentals=0,
        ),
    )(c.reshape(1), weight, pick)


def place_kernel(plan, fixed, axis, i_ref, *refs):
    out = refs[-1]
    index = i_ref[0]
    for ref, (k, moves) in zip(refs, plan):
        for start, size, base, stride in moves:
            to = base + (index ^ k) * stride
            if stride:
                to = pl.multiple_of(to, 16 if axis == 0 else 128)
            if axis == 0:
                out[pl.ds(to, size), :] = ref[start : start + size, :].astype(out.dtype)
            else:
                out[:, pl.ds(to, size)] = ref[:, start : start + size].astype(out.dtype)
    for start, size, base in fixed:
        out[:, base : base + size] = refs[len(plan)][:, start : start + size]


def place(pieces, index, shape, axis, dtype, extra=None, fixed=(), blocks=0):
    arrays = [array for array, _, _ in pieces]
    plan = [(k, moves) for _, k, moves in pieces]
    if axis == 1:
        tile = shape[0] // blocks if blocks else row_tile(shape[0])
        grid = shape[0] // tile
        block = lambda array: (tile, array.shape[1])
        at = lambda i: (i, 0)
        out_block = (tile, shape[1])
    else:
        tile = next(t for t in (384, 256, 128, shape[1]) if shape[1] % t == 0)
        grid = shape[1] // tile
        block = lambda array: (array.shape[0], tile)
        at = lambda i: (0, i)
        out_block = (shape[0], tile)
    ats = [at] * len(plan)
    if blocks:
        ats = [lambda i, k=k: (i ^ k, 0) for k, _ in plan]
    if extra is not None:
        arrays.append(extra)
        ats.append(at)
    return pl.pallas_call(
        functools.partial(place_kernel, plan, fixed, axis),
        out_shape=jax.ShapeDtypeStruct(shape, dtype),
        grid=(grid,),
        in_specs=[pl.BlockSpec(memory_space=pltpu.SMEM)]
        + [pl.BlockSpec(block(array), place_) for array, place_ in zip(arrays, ats)],
        out_specs=pl.BlockSpec(out_block, at),
        compiler_params=pltpu.CompilerParams(vmem_limit_bytes=32 * 2**20),
        cost_estimate=pl.CostEstimate(
            flops=0, bytes_accessed=6 * shape[0] * shape[1], transcendentals=0
        ),
    )(index.reshape(1), *arrays)


def add_rows_kernel(moves, first_ref, second_ref, out_ref):
    for start, size, to in moves:
        total = first_ref[start : start + size, :].astype(wide)
        total += second_ref[start : start + size, :].astype(wide)
        out_ref[to : to + size, :] = total.astype(out_ref.dtype)


def add_rows(first, second, moves):
    rows, cols = first.shape
    tile = next(t for t in (384, 256, 128) if cols % t == 0)
    spec = pl.BlockSpec((rows, tile), lambda i: (0, i))
    return pl.pallas_call(
        functools.partial(add_rows_kernel, moves),
        out_shape=jax.ShapeDtypeStruct((rows, cols), first.dtype),
        grid=(cols // tile,),
        in_specs=[spec, spec],
        out_specs=spec,
        compiler_params=pltpu.CompilerParams(vmem_limit_bytes=32 * 2**20),
        cost_estimate=pl.CostEstimate(
            flops=rows * cols, bytes_accessed=6 * rows * cols, transcendentals=0
        ),
    )(first, second)


def split_columns_kernel(size, cut, c_ref, ref, *outs):
    c = c_ref[0]
    for k in range(len(outs) // 2):
        start = pl.multiple_of((c ^ k) * size, 128)
        outs[2 * k][...] = ref[:, pl.ds(start, cut)]
        outs[2 * k + 1][...] = ref[:, pl.ds(start + cut, size - cut)]


def split_columns(array, c, count, cut):
    rows, cols = array.shape
    tile, size = rows // count, cols // count
    shapes = [(rows, cut), (rows, size - cut)] * count
    return pl.pallas_call(
        functools.partial(split_columns_kernel, size, cut),
        out_shape=[jax.ShapeDtypeStruct(shape, array.dtype) for shape in shapes],
        grid=(count,),
        in_specs=[
            pl.BlockSpec(memory_space=pltpu.SMEM),
            pl.BlockSpec((tile, cols), lambda i: (i, 0)),
        ],
        out_specs=[
            pl.BlockSpec((tile, shape[1]), lambda i, k=n // 2: (i ^ k, 0))
            for n, shape in enumerate(shapes)
        ],
        compiler_params=pltpu.CompilerParams(vmem_limit_bytes=32 * 2**20),
        cost_estimate=pl.CostEstimate(
            flops=0, bytes_accessed=4 * rows * cols, transcendentals=0
        ),
    )(c.reshape(1), array)


def join_kernel(plan, *refs):
    out = refs[-1]
    for ref, (k, first) in zip(refs, plan):
        out[k, :, first : first + ref.shape[1]] = ref[...]


def join(pieces):
    rows, width = pieces[0][0].shape
    count = 1 + max(k for _, k, _ in pieces)
    if any(array.shape[1] % 128 for array, _, _ in pieces) or rows % 64:
        blocks = [[] for _ in range(count)]
        for array, k, _ in pieces:
            blocks[k].append(array)
        return jnp.concatenate([jnp.concatenate(b, axis=1) for b in blocks], axis=0)
    joined = pl.pallas_call(
        functools.partial(join_kernel, [(k, first) for _, k, first in pieces]),
        out_shape=jax.ShapeDtypeStruct((count, rows, width), pieces[0][0].dtype),
        grid=(rows // 64,),
        in_specs=[pl.BlockSpec((64, array.shape[1]), lambda i: (i, 0)) for array, _, _ in pieces],
        out_specs=pl.BlockSpec((count, 64, width), lambda i: (0, i, 0)),
        compiler_params=pltpu.CompilerParams(vmem_limit_bytes=32 * 2**20),
        cost_estimate=pl.CostEstimate(
            flops=0, bytes_accessed=4 * count * rows * width, transcendentals=0
        ),
    )(*[array for array, _, _ in pieces])
    return joined.reshape(count * rows, width)


def turn(vectors, cosine, sine):
    half = cosine.shape[1]
    parts = []
    for start in range(0, vectors.shape[1], 2 * half):
        first = vectors[:, start : start + half]
        second = vectors[:, start + half : start + 2 * half]
        parts += [first * cosine - second * sine, second * cosine + first * sine]
    return jnp.concatenate(parts, axis=1)


def attention_back_kernel(
    heads, scale, grad_ref, query_ref, key_ref, value_ref, row_ref, column_ref,
    cosine_ref, sine_ref, all_cosine_ref, all_sine_ref, out_ref, sums_ref,
):
    step = pl.program_id(0)
    keys, values = key_ref[...], value_ref[...]
    width = keys.shape[1]

    @pl.when(step == 0)
    def _():
        sums_ref[...] = jnp.zeros_like(sums_ref)

    allowed = column_ref[...] <= row_ref[...]
    grads = []
    for head in range(heads):
        at = slice(head * width, (head + 1) * width)
        query, grad = query_ref[:, at], grad_ref[:, at]
        bent = jnp.tanh(contract_last(query, keys) * (1.0 / soft_cap))
        weights = jnp.where(allowed, jnp.exp(soft_cap * bent), 0.0)
        probs = weights * (1.0 / jnp.sum(weights, axis=1, keepdims=True))
        grad_probs = contract_last(grad, values)
        delta = jnp.sum(probs * grad_probs, axis=1, keepdims=True)
        grad_raw = (probs * (grad_probs - delta) * (1.0 - bent * bent)).astype(low)
        grads.append(dot(grad_raw, keys))
        sums_ref[0] += contract_first(grad_raw, query)
        sums_ref[1] += contract_first(probs.astype(low), grad)
    grads = jnp.concatenate(grads, axis=1) * scale
    here = pl.ds(pl.multiple_of(step * grads.shape[0], grads.shape[0]), grads.shape[0])
    split = grads.shape[1]
    out_ref[here, :split] = turn(grads, cosine_ref[...], -sine_ref[...]).astype(low)

    @pl.when(step == pl.num_programs(0) - 1)
    def _():
        turned = turn(sums_ref[0], all_cosine_ref[...], -all_sine_ref[...])
        out_ref[:, split : split + width] = turned.astype(low)
        out_ref[:, split + width :] = sums_ref[1].astype(low)


def attention_back(grad, queries, keys, values, places, cosine, sine, scale):
    length, width = keys.shape
    heads = queries.shape[1] // width
    tile = 256
    rows = lambda cols: pl.BlockSpec((tile, cols), lambda i: (i, 0))
    whole = lambda *shape: pl.BlockSpec(shape, lambda i: (0, 0))
    half = cosine.shape[1]
    return pl.pallas_call(
        functools.partial(attention_back_kernel, heads, scale),
        out_shape=jax.ShapeDtypeStruct((length, (heads + 2) * width), low),
        grid=(length // tile,),
        in_specs=[
            rows(heads * width),
            rows(heads * width),
            whole(length, width),
            whole(length, width),
            rows(1),
            whole(1, length),
            rows(half),
            rows(half),
            whole(length, half),
            whole(length, half),
        ],
        out_specs=whole(length, (heads + 2) * width),
        scratch_shapes=[pltpu.VMEM((2, length, width), wide)],
        compiler_params=pltpu.CompilerParams(vmem_limit_bytes=48 * 2**20),
        cost_estimate=pl.CostEstimate(
            flops=20 * heads * length * length * width,
            bytes_accessed=16 * length * width,
            transcendentals=2 * heads * length * length,
        ),
    )(
        grad,
        queries,
        keys,
        values,
        places[:, None],
        places[None, :],
        cosine,
        sine,
        cosine,
        sine,
    )


def column_tile(cols):
    return next(t for t in (256, 128, cols) if cols % t == 0)


def row_chunks(rows, body):
    size = next(t for t in (512, 256, 128, rows) if rows % t == 0)

    def step(i, carry):
        body(pl.ds(pl.multiple_of(i * size, size), size))
        return carry

    lax.fori_loop(0, rows // size, step, 0)


def units_kernel(x_ref, gate_ref, up_ref, hidden_ref, gate_slope_ref, up_slope_ref):
    root = (2.0 / jnp.pi) ** 0.5

    def body(at):
        x = x_ref[at, :]
        gate = dot(x, gate_ref[...])
        up = dot(x, up_ref[...])
        square = gate * gate
        bend = jnp.tanh(root * gate * (1.0 + 0.044715 * square))
        half = 0.5 * (1.0 + bend)
        activated = gate * half
        slope = half + 0.5 * gate * (1.0 - bend * bend) * root * (1.0 + 3.0 * 0.044715 * square)
        hidden_ref[at, :] = (activated * up).astype(low)
        gate_slope_ref[at, :] = (up * slope).astype(low)
        up_slope_ref[at, :] = activated.astype(low)

    row_chunks(x_ref.shape[0], body)


def units_forward(x, weights):
    rows, depth = x.shape
    cols = weights.shape[1] // 2
    tile = column_tile(cols)
    steps = cols // tile
    out = jax.ShapeDtypeStruct((rows, cols), low)
    out_spec = pl.BlockSpec((rows, tile), lambda j: (0, j))
    return pl.pallas_call(
        units_kernel,
        out_shape=[out] * 3,
        grid=(steps,),
        in_specs=[
            pl.BlockSpec((rows, depth), lambda j: (0, 0)),
            pl.BlockSpec((depth, tile), lambda j: (0, j)),
            pl.BlockSpec((depth, tile), lambda j: (0, j + steps)),
        ],
        out_specs=[out_spec] * 3,
        compiler_params=pltpu.CompilerParams(vmem_limit_bytes=48 * 2**20),
        cost_estimate=pl.CostEstimate(
            flops=4 * rows * depth * cols,
            bytes_accessed=4 * depth * cols + 2 * rows * depth + 6 * rows * cols,
            transcendentals=rows * cols,
        ),
    )(x, weights, weights)


def units_back_kernel(count, *refs):
    grads, weights = refs[:count], refs[count : 2 * count]
    gate_slope_ref, up_slope_ref, gate_ref, up_ref = refs[2 * count :]
    cols = gate_slope_ref.shape[1]
    tile = column_tile(cols)

    def step(j, carry):
        at = pl.ds(pl.multiple_of(j * tile, tile), tile)
        grad = sum(contract_last(g[...], w[at, :]) for g, w in zip(grads, weights))
        gate_ref[:, at] = (grad * gate_slope_ref[:, at].astype(wide)).astype(low)
        up_ref[:, at] = (grad * up_slope_ref[:, at].astype(wide)).astype(low)
        return carry

    lax.fori_loop(0, cols // tile, step, 0)


def units_back(grads, weights, gate_slope, up_slope):
    rows, cols = gate_slope.shape
    tile = next(t for t in (512, 256, 128, rows) if rows % t == 0)
    width = sum(g.shape[1] for g in grads)
    return pl.pallas_call(
        functools.partial(units_back_kernel, len(grads)),
        out_shape=[jax.ShapeDtypeStruct((rows, cols), low)] * 2,
        grid=(rows // tile,),
        in_specs=[pl.BlockSpec((tile, g.shape[1]), lambda i: (i, 0)) for g in grads]
        + [pl.BlockSpec(w.shape, lambda i: (0, 0)) for w in weights]
        + [pl.BlockSpec((tile, cols), lambda i: (i, 0))] * 2,
        out_specs=[pl.BlockSpec((tile, cols), lambda i: (i, 0))] * 2,
        compiler_params=pltpu.CompilerParams(vmem_limit_bytes=56 * 2**20),
        cost_estimate=pl.CostEstimate(
            flops=2 * rows * width * cols,
            bytes_accessed=2 * width * cols + 2 * rows * width + 8 * rows * cols,
            transcendentals=0,
        ),
    )(*grads, *weights, gate_slope, up_slope)


def product_kernel(*refs):
    *lefts, right_ref, out_ref = refs
    depth = lefts[0].shape[1]

    def body(at):
        total = sum(
            contract_last(left[at, :], right_ref[:, i * depth : (i + 1) * depth])
            for i, left in enumerate(lefts)
        )
        out_ref[at, :] = total.astype(out_ref.dtype)

    row_chunks(lefts[0].shape[0], body)


def product_last(lefts, right):
    rows, depth = lefts[0].shape
    cols, width = right.shape
    tile = column_tile(cols)
    return pl.pallas_call(
        product_kernel,
        out_shape=jax.ShapeDtypeStruct((rows, cols), low),
        grid=(cols // tile,),
        in_specs=[pl.BlockSpec((rows, depth), lambda j: (0, 0)) for _ in lefts]
        + [pl.BlockSpec((tile, width), lambda j: (j, 0))],
        out_specs=pl.BlockSpec((rows, tile), lambda j: (0, j)),
        compiler_params=pltpu.CompilerParams(vmem_limit_bytes=48 * 2**20),
        cost_estimate=pl.CostEstimate(
            flops=2 * rows * width * cols,
            bytes_accessed=2 * (rows * width + width * cols + rows * cols),
            transcendentals=0,
        ),
    )(*lefts, right)


def cores_apart_kernel(count, x_ref, out_ref):
    part = x_ref.shape[1] // count
    order = [*range(0, count, 2), *range(1, count, 2)]
    out_ref[...] = jnp.concatenate(
        [x_ref[:, b * part : (b + 1) * part] for b in order], axis=1
    )


def cores_apart(x, count):
    rows, cols = x.shape
    return pl.pallas_call(
        functools.partial(cores_apart_kernel, count),
        out_shape=jax.ShapeDtypeStruct(x.shape, x.dtype),
        grid=(rows // 128,),
        in_specs=[pl.BlockSpec((128, cols), lambda i: (i, 0))],
        out_specs=pl.BlockSpec((128, cols), lambda i: (i, 0)),
        compiler_params=pltpu.CompilerParams(vmem_limit_bytes=32 * 2**20),
        cost_estimate=pl.CostEstimate(
            flops=0, bytes_accessed=4 * rows * cols, transcendentals=0
        ),
    )(x)


def frequencies(half, head_dim):
    return rope_base ** (-(jnp.arange(half, dtype=wide) * 2.0) / head_dim)


def rotate(vectors, cosine, sine):
    half = vectors.shape[-1] // 2
    first = vectors[..., :half]
    second = vectors[..., half:]
    return jnp.concatenate(
        [first * cosine - second * sine, second * cosine + first * sine], axis=-1
    )


def inverse_rms(vectors):
    return lax.rsqrt(jnp.mean(vectors * vectors, axis=-1, keepdims=True) + epsilon)


def norm_back(vectors, inverse, gain, upstream):
    scaled = upstream * gain
    unit = vectors * inverse
    grad_vectors = inverse * (scaled - unit * jnp.mean(unit * scaled, axis=-1, keepdims=True))
    return (grad_vectors, jnp.sum(upstream * unit, axis=0))


def dot(left, right):
    return jnp.dot(left, right, preferred_element_type=wide)


def contract_last(left, right):
    return lax.dot_general(left, right, (((1,), (1,)), ((), ())), preferred_element_type=wide)


def contract_first(left, right):
    return lax.dot_general(left, right, (((0,), (0,)), ((), ())), preferred_element_type=wide)


def per_device(
    inputs,
    positions,
    pre_attn_gain,
    post_attn_gain,
    pre_mlp_gain,
    post_mlp_gain,
    query_weight,
    key_weight,
    value_weight,
    out_weight,
    gate_weight,
    up_weight,
    down_weight,
    cotangent,
):
    n_ctx, n_fsdp = lax.axis_size("ctx"), lax.axis_size("fsdp")
    c, f = lax.axis_index("ctx"), lax.axis_index("fsdp")
    rows = inputs[0].astype(wide)
    tokens, width = rows.shape
    length = n_ctx * tokens
    scale = HD ** (-0.5)
    my_heads = HQ // n_ctx
    my_kv = max(KV // n_ctx, 1)
    share = max(n_ctx // KV, 1)
    groups = my_heads // my_kv
    kv_start = (c // share) * my_kv * HD
    query_cols, kv_cols = my_heads * HD, my_kv * HD
    out_cols = width // n_ctx
    ff_rows = down_weight.shape[0]
    part = ff_rows // n_ctx
    main = ff_rows // 128 // n_ctx * 128
    rest = part - main
    chips = n_fsdp // 2
    tiled = ff_rows % 128 == 0 and main > 0 and rest * n_ctx == 128 and rest % 16 == 0
    tiled = tiled and chips * rest % 128 == 0 and query_cols % 256 == 0
    last_cols = width // 384 * 128

    def gathered(shard):
        return lax.all_gather(shard, "fsdp", axis=0, tiled=True)

    def units_together(full):
        if not tiled:
            return full
        moves = []
        for block in range(n_fsdp):
            to = unit_place(block, n_fsdp, main, rest)
            moves.append((block * part, main, to, 0))
            to = rest_place(block % 2, n_fsdp, main, rest) + block // 2 * rest
            moves.append((block * part + main, rest, to, 0))
        return place([(full, 0, moves)], jnp.zeros((), jnp.int32), full.shape, 0, full.dtype)

    def chip_term(term):
        return chip_sum(term.astype(low))

    def unit_term(left, right):
        if not tiled:
            return chip_term(contract_first(left, right))
        half, core = chips * part, f & 1
        theirs = lax.dynamic_slice_in_dim(left, (1 - core) * half, half, 1)
        theirs = swap(contract_first(theirs, right).astype(low), "fsdp", 1)
        mine = contract_first(lax.dynamic_slice_in_dim(left, core * half, half, 1), right)
        moves = [(chip * main, main, chip * part) for chip in range(chips)]
        moves += [
            (chips * main + chip * rest, rest, chip * part + main) for chip in range(chips)
        ]
        return add_rows(mine.astype(low), theirs, moves)

    def weight_term(left, right):
        if not tiled:
            return chip_term(contract_first(left, right))
        half, core = left.shape[1] // 2, f & 1
        theirs = lax.dynamic_slice_in_dim(left, (1 - core) * half, half, 1)
        theirs = swap(contract_first(theirs, right).astype(low), "fsdp", 1)
        mine = contract_first(lax.dynamic_slice_in_dim(left, core * half, half, 1), right)
        return (mine + theirs.astype(wide)).astype(low)

    def my_units(weight):
        if tiled:
            return take_units(weight, c, n_fsdp, main, rest)
        split = weight.reshape(weight.shape[0], n_fsdp, n_ctx, part)
        return lax.dynamic_index_in_dim(split, c, 2, keepdims=False).reshape(
            weight.shape[0], n_fsdp * part
        )

    def in_order(blocks):
        blocks = list(blocks)
        for bit in range(n_ctx.bit_length() - 1):
            mask = 1 << bit
            odd = (c & mask) != 0
            blocks = [jnp.where(odd, blocks[k ^ mask], blocks[k]) for k in range(n_ctx)]
        return blocks

    def token_blocks(array):
        return [array[k * tokens : (k + 1) * tokens] for k in range(n_ctx)]

    def block_order(blocks, k):
        pieces = blocks.reshape(n_ctx, tokens, blocks.shape[-1])
        return jnp.concatenate([pieces[k ^ m] for m in range(n_ctx)], axis=0)

    def from_columns(array):
        got = jnp.stack(exchange(token_blocks(array)))
        return jnp.transpose(jnp.take(got, jnp.arange(n_ctx) ^ c, axis=0), (1, 0, 2)).reshape(
            tokens, width
        )

    def to_columns(array):
        split = array.reshape(tokens, n_ctx, out_cols)
        split = jnp.take(split, jnp.arange(n_ctx) ^ c, axis=1)
        return jnp.concatenate(exchange([split[:, k] for k in range(n_ctx)]), axis=0)

    my_qkv = jnp.concatenate(
        [
            lax.dynamic_slice_in_dim(query_weight, c * query_cols, query_cols, 1),
            lax.dynamic_slice_in_dim(key_weight, kv_start, kv_cols, 1),
            lax.dynamic_slice_in_dim(value_weight, kv_start, kv_cols, 1),
        ],
        axis=1,
    )
    full_qkv = gathered(my_qkv)
    full_out = gathered(lax.dynamic_slice_in_dim(out_weight, c * out_cols, out_cols, 1))
    full_units = gathered(jnp.concatenate([my_units(gate_weight), my_units(up_weight)], axis=1))
    if tiled:
        my_down = jnp.concatenate(
            [
                lax.dynamic_slice_in_dim(down_weight, c * main, main, 0),
                lax.dynamic_slice_in_dim(down_weight, n_ctx * main + c * rest, rest, 0),
            ],
            axis=0,
        )
    else:
        my_down = lax.dynamic_slice_in_dim(down_weight, c * part, part, 0)
    gains = jnp.stack([pre_attn_gain, post_attn_gain, pre_mlp_gain, post_mlp_gain])
    gains = jnp.stack([gains if k == 0 else swap(gains, "fsdp", k) for k in range(n_fsdp)])
    gains = jnp.take(gains, jnp.arange(n_fsdp) ^ f, axis=0)
    gains = jnp.transpose(gains, (1, 0, 2)).reshape(4, width).astype(wide)
    gain_a, gain_b, gain_c, gain_d = gains[0], gains[1], gains[2], gains[3]

    inverse_a = inverse_rms(rows)
    normed = join(gather_pieces((rows * inverse_a * gain_a).astype(low)))
    normed_apart = cores_apart(normed, n_fsdp) if tiled else normed
    places = jnp.concatenate(gather_blocks(positions[0], halves=False), axis=0)
    angles = places.astype(wide)[:, None] * frequencies(HD // 2, HD)
    cosine, sine = jnp.cos(angles), jnp.sin(angles)
    projected = dot(normed, full_qkv)
    query_lin = projected[:, :query_cols].reshape(length, my_heads, HD)
    key_lin = projected[:, query_cols : query_cols + kv_cols].reshape(length, my_kv, HD)
    values = projected[:, query_cols + kv_cols :].astype(low).reshape(length, my_kv, HD)
    queries = (rotate(query_lin, cosine[:, None], sine[:, None]) * scale).astype(low)
    keys = rotate(key_lin, cosine[:, None], sine[:, None]).astype(low)
    queries = queries.reshape(length, my_kv, groups, HD)
    allowed = places[None, :] <= places[:, None]
    raw = jnp.einsum("tkgd,rkd->kgtr", queries, keys, preferred_element_type=wide)
    bent = jnp.tanh(raw / soft_cap)
    weights = jnp.where(allowed, jnp.exp(soft_cap * bent), 0.0)
    total = jnp.sum(weights, axis=-1)
    mixed = jnp.einsum("kgtr,rkd->kgtd", weights.astype(low), values, preferred_element_type=wide)
    mixed = mixed / total[..., None]
    attn = jnp.transpose(mixed, (2, 0, 1, 3)).reshape(length, query_cols).astype(low)

    if tiled:
        pieces = [
            (array, k, [(0, array.shape[1], first, query_cols)])
            for array, k, first in gather_pieces(attn)
        ]
        attn_all = place(pieces, c, (length, HQ * HD), 1, low, blocks=n_ctx)
    else:
        attn_blocks = [block_order(block, k) for k, block in enumerate(gather_blocks(attn))]
        attn_all = jnp.concatenate(in_order(attn_blocks), axis=1)
    branch = from_columns(dot(attn_all, full_out).astype(low)).astype(wide)
    inverse_b = inverse_rms(branch)
    middle = rows + branch * inverse_b * gain_b
    inverse_c = inverse_rms(middle)

    normed_mlp = join(gather_pieces((middle * inverse_c * gain_c).astype(low)))
    normed_mlp_apart = cores_apart(normed_mlp, n_fsdp) if tiled else normed_mlp
    my_down = after(my_down, full_units, normed_mlp_apart)
    first_down, last_down = gathered(my_down[:, :-last_cols]), my_down[:, -last_cols:]
    hidden, gate_slope, up_slope = units_forward(normed_mlp, full_units)
    last_down = gathered(after(last_down, first_down, hidden))
    full_downs = [units_together(first_down), units_together(last_down)]
    first_terms, last_terms = (
        token_blocks(dot(hidden, full).astype(low)) for full in full_downs
    )
    last_terms = sum(term.astype(wide) for term in exchange(last_terms))
    down = jnp.concatenate([scatter_sum(halved(first_terms)), last_terms], axis=1)
    inverse_d = inverse_rms(down)
    output = (middle + down * inverse_d * gain_d).astype(low)[None]

    grad_result = cotangent[0].astype(wide)
    grad_down, grad_gain_d = norm_back(down, inverse_d, gain_d, grad_result)
    grad_down = grad_down.astype(low)
    pieces = gather_pieces(grad_down[:, -last_cols:])
    grad_downs = [join(pieces)]
    down_terms = [unit_term(hidden, grad_downs[0])]
    others = [array for array, _, _ in pieces[1:3]]
    pieces = gather_pieces(after(grad_down[:, :-last_cols], *others))
    pieces[0] = (after(pieces[0][0], down_terms[0]), *pieces[0][1:])
    grad_downs.append(join(pieces))
    down_terms.append(unit_term(hidden, grad_downs[1]))
    grad_downs, down_terms[1] = lax.optimization_barrier((grad_downs, down_terms[1]))
    down_sums = [fsdp_sum(term) for term in down_terms]
    grad_gate, grad_up = units_back(grad_downs, full_downs[::-1], gate_slope, up_slope)
    grad_normed_mlp = product_last([grad_gate, grad_up], full_units)
    grad_normed_mlp, grad_gate = lax.optimization_barrier((grad_normed_mlp, grad_gate))
    gate_term = weight_term(normed_mlp_apart, after(grad_gate, down_sums[0]))
    gate_sum = fsdp_sum(gate_term)
    up_term = weight_term(normed_mlp_apart, after(grad_up, gate_term))
    up_sum = fsdp_sum(up_term)
    grad_normed_mlp = scatter_sum(halved(token_blocks(grad_normed_mlp)))
    down_pieces = [gather_pieces(after(down_sums[0], grad_gate))]
    arrived = [piece[0] for piece in down_pieces[0]]
    grad_normed_mlp = after(grad_normed_mlp, up_term, down_sums[1], *arrived)
    down_pieces.append(gather_pieces(after(down_sums[1], grad_normed_mlp)))
    grad_middle_mlp, grad_gain_c = norm_back(middle, inverse_c, gain_c, grad_normed_mlp)
    grad_middle = grad_result + grad_middle_mlp
    grad_branch, grad_gain_b = norm_back(branch, inverse_b, gain_b, grad_middle)

    arrived = [piece[0] for piece in down_pieces[1][1:3]]
    grad_branch_cols = to_columns(after(grad_branch.astype(low), *arrived))
    out_term = chip_term(contract_first(attn_all, grad_branch_cols))
    grad_attn_all = contract_last(grad_branch_cols, full_out).astype(low)
    if tiled:
        parts = split_columns(grad_attn_all, c, n_ctx, cut_at(query_cols))
        grad_attn = scatter_sum(list(zip(parts[::2], parts[1::2]))).astype(low)
    else:
        parts = [
            lax.dynamic_slice_in_dim(grad_attn_all, (c ^ k) * query_cols, query_cols, 1)
            for k in range(n_ctx)
        ]
        parts = [block_order(part_, k) for k, part_ in enumerate(parts)]
        grad_attn = scatter_sum(halved(parts)).astype(low)
    grad_attn = after(grad_attn, gate_sum, *[piece[0] for piece in down_pieces[1]])
    grad_projected = attention_back(
        grad_attn,
        queries.reshape(length, query_cols),
        keys.reshape(length, kv_cols),
        values.reshape(length, kv_cols),
        places,
        cosine,
        sine,
        scale,
    )
    qkv_term = weight_term(normed_apart, grad_projected)
    pad = (qkv_term.shape[0] - out_term.shape[0]) // chips
    out_term = jnp.pad(out_term.reshape(chips, -1, out_cols), ((0, 0), (0, pad), (0, 0)))
    out_term = out_term.reshape(qkv_term.shape[0], out_cols)
    attn_sum = fsdp_sum(jnp.concatenate([qkv_term, out_term], axis=1))
    qkv_sum = attn_sum[:, : qkv_term.shape[1]]
    out_sum = attn_sum[: attn_sum.shape[0] - pad, qkv_term.shape[1] :]
    grad_normed = contract_last(grad_projected, full_qkv).astype(low)
    grad_normed = scatter_sum(halved(token_blocks(grad_normed)))
    grad_normed = after(grad_normed, up_sum)
    grad_rows, grad_gain_a = norm_back(rows, inverse_a, gain_a, grad_normed)
    input_grad = (grad_middle + grad_rows).astype(low)[None]

    gain_terms = jnp.stack([grad_gain_a, grad_gain_b, grad_gain_c, grad_gain_d])
    for bit in range(n_ctx.bit_length() - 1):
        gain_terms = gain_terms + swap(gain_terms, "ctx", 1 << bit)
    gain_terms = jnp.transpose(gain_terms.reshape(4, n_fsdp, width // n_fsdp), (1, 0, 2))
    gain_terms = jnp.take(gain_terms, jnp.arange(n_fsdp) ^ f, axis=0)
    gain_sums = gain_terms[0]
    for k in range(1, n_fsdp):
        gain_sums = gain_sums + swap(gain_terms[k], "fsdp", k)

    if share == 1:
        qkv_pieces = gather_pieces(qkv_sum)

        def columns_of(first, size, shape):
            pieces = []
            for array, k, start in qkv_pieces:
                begin, end = max(first, start), min(first + size, start + array.shape[1])
                if begin < end:
                    pieces.append((array, k, [(begin - start, size, 0, size)]))
            return place(pieces, c, shape, 1, wide)

        query_grad = columns_of(0, query_cols, query_weight.shape)
        key_grad = columns_of(query_cols, kv_cols, key_weight.shape)
        value_grad = columns_of(query_cols + kv_cols, kv_cols, value_weight.shape)
    else:
        qkv_blocks = gather_blocks(qkv_sum)
        query_grad = jnp.zeros(query_weight.shape, wide)
        key_grad = jnp.zeros(key_weight.shape, wide)
        value_grad = jnp.zeros(value_weight.shape, wide)
        for k, block in enumerate(qkv_blocks):
            query_grad = lax.dynamic_update_slice_in_dim(
                query_grad, block[:, :query_cols].astype(wide), (c ^ k) * query_cols, 1
            )
        for k in range(0, n_ctx, share):
            block = sum(qkv_blocks[k + s][:, query_cols:].astype(wide) for s in range(share))
            start = ((c ^ k) // share) * kv_cols
            key_grad = lax.dynamic_update_slice_in_dim(key_grad, block[:, :kv_cols], start, 1)
            value_grad = lax.dynamic_update_slice_in_dim(value_grad, block[:, kv_cols:], start, 1)

    out_grad = jnp.concatenate(in_order(gather_blocks(out_sum)), axis=1).astype(wide)

    def all_units(total):
        if not tiled:
            blocks = gather_blocks(total)
            blocks = [b.reshape(b.shape[0], n_fsdp, part) for b in in_order(blocks)]
            return jnp.stack(blocks, axis=2).reshape(gate_weight.shape).astype(wide)
        pieces, tails = [], []
        for array, k, start in gather_pieces(total):
            moves = []
            for b in range(n_fsdp):
                begin = unit_place(b, n_fsdp, main, rest) - start
                if 0 <= begin < array.shape[1]:
                    moves.append((begin, main, b * ff_rows, main))
            pieces.append((array, k, moves))
            for core in (0, 1):
                begin = rest_place(core, n_fsdp, main, rest) - start
                if 0 <= begin < array.shape[1]:
                    tails.append((k, core, array[:, begin : begin + chips * rest]))
        tails = [tail for _, _, tail in sorted(tails, key=lambda item: item[:2])]
        source = jnp.arange(n_ctx * n_fsdp * rest)[:, None]
        index, unit = source // (n_fsdp * rest), source % (n_fsdp * rest)
        block = unit // rest % chips * 2 + unit // (chips * rest)
        target = block * 128 + (c ^ index) * rest + unit % rest
        spread_to = (target == jnp.arange(n_fsdp * 128)[None, :]).astype(low)
        return place(
            pieces,
            c,
            gate_weight.shape,
            1,
            wide,
            dot(jnp.concatenate(tails, axis=1), spread_to),
            [(b * 128, 128, (b + 1) * ff_rows - 128) for b in range(n_fsdp)],
        )

    gate_grad = all_units(after(gate_sum, qkv_term))
    up_grad = all_units(up_sum)
    down_halves = zip(*[as_blocks(pieces) for pieces in down_pieces[::-1]])
    down_blocks = [jnp.concatenate(block, axis=1) for block in down_halves]
    down_blocks[0] = after(down_blocks[0], qkv_term)
    if tiled:
        moves = [(0, main, 0, main), (main, rest, n_ctx * main, rest)]
        pieces = [(block, k, moves) for k, block in enumerate(down_blocks)]
        down_grad = place(pieces, c, down_weight.shape, 0, wide)
    else:
        down_grad = jnp.concatenate(in_order(down_blocks), axis=0).astype(wide)
    return (
        output,
        input_grad,
        gain_sums[0],
        gain_sums[1],
        gain_sums[2],
        gain_sums[3],
        query_grad,
        key_grad,
        value_grad,
        out_grad,
        gate_grad,
        up_grad,
        down_grad,
    )


def solution(mesh):
    return jax.shard_map(
        per_device,
        mesh=mesh,
        in_specs=(
            P("fsdp", "ctx", None),
            P("fsdp", "ctx"),
            P("fsdp"),
            P("fsdp"),
            P("fsdp"),
            P("fsdp"),
            P("fsdp", None),
            P("fsdp", None),
            P("fsdp", None),
            P("fsdp", None),
            P("fsdp", None),
            P("fsdp", None),
            P("fsdp", None),
            P("fsdp", "ctx", None),
        ),
        out_specs=(
            P("fsdp", "ctx", None),
            P("fsdp", "ctx", None),
            P("fsdp"),
            P("fsdp"),
            P("fsdp"),
            P("fsdp"),
            P("fsdp", None),
            P("fsdp", None),
            P("fsdp", None),
            P("fsdp", None),
            P("fsdp", None),
            P("fsdp", None),
            P("fsdp", None),
        ),
        check_vma=False,
    )
```

```python
import functools

import jax
import jax.numpy as jnp
from jax import lax
from jax.experimental import pallas as pl
from jax.experimental.pallas import tpu as pltpu
from jax.sharding import PartitionSpec as P

HQ = 8
KV = 4
HD = 256

soft_cap = 50.0
epsilon = 1e-06
rope_base = 10000.0
low = jnp.bfloat16
wide = jnp.float32


def swap(shard, axis, mask):
    size = lax.axis_size(axis)
    return lax.ppermute(shard, axis, [(i, i ^ mask) for i in range(size)])


def after(value, *others):
    return lax.optimization_barrier((value, *others))[0]


def chip_groups():
    size = lax.axis_size("fsdp")
    return [list(range(core, size, 2)) for core in (0, 1)]


def cut_at(width):
    return (width // 512) * 256 if width >= 512 else width // 2


def gather_pieces(block, halves=True):
    width = block.shape[-1]
    got, pieces = {0: block}, [(block, 0, 0)]
    for k in range(1, lax.axis_size("ctx")):
        low_bit, high_bit = k & -k, 1 << (k.bit_length() - 1)
        if low_bit == high_bit or not halves:
            got[k] = swap(got[k ^ high_bit], "ctx", high_bit)
            pieces.append((got[k], k, 0))
        else:
            cut = cut_at(width)
            first = swap(got[k ^ high_bit][..., :cut], "ctx", high_bit)
            second = swap(got[k ^ low_bit][..., cut:], "ctx", low_bit)
            pieces += [(first, k, 0), (second, k, cut)]
            if k + 1 < lax.axis_size("ctx"):
                got[k] = jnp.concatenate([first, second], axis=-1)
    return pieces


def gather_blocks(block, halves=True):
    return as_blocks(gather_pieces(block, halves))


def as_blocks(pieces):
    blocks = [[] for _ in range(lax.axis_size("ctx"))]
    for array, k, _ in pieces:
        blocks[k].append(array)
    return [b[0] if len(b) == 1 else jnp.concatenate(b, axis=-1) for b in blocks]


def halved(parts):
    cut = cut_at(parts[0].shape[-1])
    return [(part[..., :cut], part[..., cut:]) for part in parts]


def scatter_sum(terms):
    terms = list(terms)
    for k in range(len(terms) - 1, 0, -1):
        low_bit, high_bit = k & -k, 1 << (k.bit_length() - 1)
        first = swap(terms[k][0], "ctx", high_bit).astype(wide)
        second = swap(terms[k][1], "ctx", low_bit).astype(wide)
        to_first, to_second = k ^ high_bit, k ^ low_bit
        first = terms[to_first][0].astype(wide) + first
        terms[to_first] = (first.astype(low) if to_first else first, terms[to_first][1])
        second = terms[to_second][1].astype(wide) + second
        terms[to_second] = (terms[to_second][0], second.astype(low) if to_second else second)
    return jnp.concatenate(terms[0], axis=-1)


def exchange(parts):
    return [parts[0]] + [swap(part, "ctx", k) for k, part in enumerate(parts) if k]


def chip_sum(term):
    count = lax.axis_size("fsdp")
    core = lax.axis_index("fsdp") & 1
    halves = term.reshape(count // 2, 2, term.shape[0] // count, term.shape[1])
    theirs = swap(lax.dynamic_index_in_dim(halves, 1 - core, 1, keepdims=False), "fsdp", 1)
    mine = lax.dynamic_index_in_dim(halves, core, 1, keepdims=False)
    total = (mine.astype(wide) + theirs.astype(wide)).astype(low)
    return total.reshape(-1, term.shape[1])


def fsdp_sum(arr):
    return lax.psum_scatter(
        arr,
        "fsdp",
        scatter_dimension=0,
        tiled=True,
        axis_index_groups=chip_groups(),
    )


def row_tile(rows):
    return next(t for t in (48, 32, 16, rows) if rows % t == 0)


def unit_place(block, count, main, rest):
    return block % 2 * (count // 2) * (main + rest) + block // 2 * main


def rest_place(core, count, main, rest):
    return core * (count // 2) * (main + rest) + count // 2 * main


def take_units_kernel(count, cols, main, rest, c_ref, weight_ref, pick_ref, out_ref):
    c = c_ref[0]
    for b in range(count):
        start = pl.multiple_of(b * cols + c * main, 128)
        to = unit_place(b, count, main, rest)
        out_ref[:, to : to + main] = weight_ref[:, pl.ds(start, main)]
    last = jnp.concatenate(
        [weight_ref[:, (b + 1) * cols - 128 : (b + 1) * cols] for b in range(count)], axis=1
    )
    picked = jnp.dot(last, pick_ref[...], preferred_element_type=jnp.float32)
    size = count // 2 * rest
    for core in (0, 1):
        to = rest_place(core, count, main, rest)
        out_ref[:, to : to + size] = picked[:, core * size : (core + 1) * size].astype(out_ref.dtype)


def take_units(weight, c, count, main, rest):
    rows, cols = weight.shape
    source = jnp.arange(count * 128)[:, None]
    target = jnp.arange(count * rest)[None, :]
    block = target // rest % (count // 2) * 2 + target // (count // 2 * rest)
    pick = (source == block * 128 + c * rest + target % rest).astype(weight.dtype)
    tile = row_tile(rows)
    return pl.pallas_call(
        functools.partial(take_units_kernel, count, cols // count, main, rest),
        out_shape=jax.ShapeDtypeStruct((rows, count * (main + rest)), weight.dtype),
        grid=(rows // tile,),
        in_specs=[
            pl.BlockSpec(memory_space=pltpu.SMEM),
            pl.BlockSpec((tile, cols), lambda i: (i, 0)),
            pl.BlockSpec(pick.shape, lambda i: (0, 0)),
        ],
        out_specs=pl.BlockSpec((tile, count * (main + rest)), lambda i: (i, 0)),
        compiler_params=pltpu.CompilerParams(vmem_limit_bytes=32 * 2**20),
        cost_estimate=pl.CostEstimate(
            flops=2 * rows * count * 128 * count * rest,
            bytes_accessed=3 * rows * cols,
            transcendentals=0,
        ),
    )(c.reshape(1), weight, pick)


def place_kernel(plan, fixed, axis, i_ref, *refs):
    out = refs[-1]
    index = i_ref[0]
    for ref, (k, moves) in zip(refs, plan):
        for start, size, base, stride in moves:
            to = base + (index ^ k) * stride
            if stride:
                to = pl.multiple_of(to, 16 if axis == 0 else 128)
            if axis == 0:
                out[pl.ds(to, size), :] = ref[start : start + size, :].astype(out.dtype)
            else:
                out[:, pl.ds(to, size)] = ref[:, start : start + size].astype(out.dtype)
    for start, size, base in fixed:
        out[:, base : base + size] = refs[len(plan)][:, start : start + size]


def place(pieces, index, shape, axis, dtype, extra=None, fixed=(), blocks=0):
    arrays = [array for array, _, _ in pieces]
    plan = [(k, moves) for _, k, moves in pieces]
    if axis == 1:
        tile = shape[0] // blocks if blocks else row_tile(shape[0])
        grid = shape[0] // tile
        block = lambda array: (tile, array.shape[1])
        at = lambda i: (i, 0)
        out_block = (tile, shape[1])
    else:
        tile = next(t for t in (384, 256, 128, shape[1]) if shape[1] % t == 0)
        grid = shape[1] // tile
        block = lambda array: (array.shape[0], tile)
        at = lambda i: (0, i)
        out_block = (shape[0], tile)
    ats = [at] * len(plan)
    if blocks:
        ats = [lambda i, k=k: (i ^ k, 0) for k, _ in plan]
    if extra is not None:
        arrays.append(extra)
        ats.append(at)
    return pl.pallas_call(
        functools.partial(place_kernel, plan, fixed, axis),
        out_shape=jax.ShapeDtypeStruct(shape, dtype),
        grid=(grid,),
        in_specs=[pl.BlockSpec(memory_space=pltpu.SMEM)]
        + [pl.BlockSpec(block(array), place_) for array, place_ in zip(arrays, ats)],
        out_specs=pl.BlockSpec(out_block, at),
        compiler_params=pltpu.CompilerParams(vmem_limit_bytes=32 * 2**20),
        cost_estimate=pl.CostEstimate(
            flops=0, bytes_accessed=6 * shape[0] * shape[1], transcendentals=0
        ),
    )(index.reshape(1), *arrays)


def add_rows_kernel(moves, first_ref, second_ref, out_ref):
    for start, size, to in moves:
        total = first_ref[start : start + size, :].astype(wide)
        total += second_ref[start : start + size, :].astype(wide)
        out_ref[to : to + size, :] = total.astype(out_ref.dtype)


def add_rows(first, second, moves):
    rows, cols = first.shape
    tile = next(t for t in (384, 256, 128) if cols % t == 0)
    spec = pl.BlockSpec((rows, tile), lambda i: (0, i))
    return pl.pallas_call(
        functools.partial(add_rows_kernel, moves),
        out_shape=jax.ShapeDtypeStruct((rows, cols), first.dtype),
        grid=(cols // tile,),
        in_specs=[spec, spec],
        out_specs=spec,
        compiler_params=pltpu.CompilerParams(vmem_limit_bytes=32 * 2**20),
        cost_estimate=pl.CostEstimate(
            flops=rows * cols, bytes_accessed=6 * rows * cols, transcendentals=0
        ),
    )(first, second)


def split_columns_kernel(size, cut, c_ref, ref, *outs):
    c = c_ref[0]
    for k in range(len(outs) // 2):
        start = pl.multiple_of((c ^ k) * size, 128)
        outs[2 * k][...] = ref[:, pl.ds(start, cut)]
        outs[2 * k + 1][...] = ref[:, pl.ds(start + cut, size - cut)]


def split_columns(array, c, count, cut):
    rows, cols = array.shape
    tile, size = rows // count, cols // count
    shapes = [(rows, cut), (rows, size - cut)] * count
    return pl.pallas_call(
        functools.partial(split_columns_kernel, size, cut),
        out_shape=[jax.ShapeDtypeStruct(shape, array.dtype) for shape in shapes],
        grid=(count,),
        in_specs=[
            pl.BlockSpec(memory_space=pltpu.SMEM),
            pl.BlockSpec((tile, cols), lambda i: (i, 0)),
        ],
        out_specs=[
            pl.BlockSpec((tile, shape[1]), lambda i, k=n // 2: (i ^ k, 0))
            for n, shape in enumerate(shapes)
        ],
        compiler_params=pltpu.CompilerParams(vmem_limit_bytes=32 * 2**20),
        cost_estimate=pl.CostEstimate(
            flops=0, bytes_accessed=4 * rows * cols, transcendentals=0
        ),
    )(c.reshape(1), array)


def join_kernel(plan, *refs):
    out = refs[-1]
    for ref, (k, first) in zip(refs, plan):
        out[k, :, first : first + ref.shape[1]] = ref[...]


def join(pieces):
    rows, width = pieces[0][0].shape
    count = 1 + max(k for _, k, _ in pieces)
    if any(array.shape[1] % 128 for array, _, _ in pieces) or rows % 64:
        blocks = [[] for _ in range(count)]
        for array, k, _ in pieces:
            blocks[k].append(array)
        return jnp.concatenate([jnp.concatenate(b, axis=1) for b in blocks], axis=0)
    joined = pl.pallas_call(
        functools.partial(join_kernel, [(k, first) for _, k, first in pieces]),
        out_shape=jax.ShapeDtypeStruct((count, rows, width), pieces[0][0].dtype),
        grid=(rows // 64,),
        in_specs=[pl.BlockSpec((64, array.shape[1]), lambda i: (i, 0)) for array, _, _ in pieces],
        out_specs=pl.BlockSpec((count, 64, width), lambda i: (0, i, 0)),
        compiler_params=pltpu.CompilerParams(vmem_limit_bytes=32 * 2**20),
        cost_estimate=pl.CostEstimate(
            flops=0, bytes_accessed=4 * count * rows * width, transcendentals=0
        ),
    )(*[array for array, _, _ in pieces])
    return joined.reshape(count * rows, width)


def turn(vectors, cosine, sine):
    half = cosine.shape[1]
    parts = []
    for start in range(0, vectors.shape[1], 2 * half):
        first = vectors[:, start : start + half]
        second = vectors[:, start + half : start + 2 * half]
        parts += [first * cosine - second * sine, second * cosine + first * sine]
    return jnp.concatenate(parts, axis=1)


def attention_back_kernel(
    heads, scale, grad_ref, query_ref, key_ref, value_ref, row_ref, column_ref,
    cosine_ref, sine_ref, all_cosine_ref, all_sine_ref, out_ref, sums_ref,
):
    step = pl.program_id(0)
    keys, values = key_ref[...], value_ref[...]
    width = keys.shape[1]

    @pl.when(step == 0)
    def _():
        sums_ref[...] = jnp.zeros_like(sums_ref)

    allowed = column_ref[...] <= row_ref[...]
    grads = []
    for head in range(heads):
        at = slice(head * width, (head + 1) * width)
        query, grad = query_ref[:, at], grad_ref[:, at]
        bent = jnp.tanh(contract_last(query, keys) * (1.0 / soft_cap))
        weights = jnp.where(allowed, jnp.exp(soft_cap * bent), 0.0)
        probs = weights * (1.0 / jnp.sum(weights, axis=1, keepdims=True))
        grad_probs = contract_last(grad, values)
        delta = jnp.sum(probs * grad_probs, axis=1, keepdims=True)
        grad_raw = (probs * (grad_probs - delta) * (1.0 - bent * bent)).astype(low)
        grads.append(dot(grad_raw, keys))
        sums_ref[0] += contract_first(grad_raw, query)
        sums_ref[1] += contract_first(probs.astype(low), grad)
    grads = jnp.concatenate(grads, axis=1) * scale
    here = pl.ds(pl.multiple_of(step * grads.shape[0], grads.shape[0]), grads.shape[0])
    split = grads.shape[1]
    out_ref[here, :split] = turn(grads, cosine_ref[...], -sine_ref[...]).astype(low)

    @pl.when(step == pl.num_programs(0) - 1)
    def _():
        turned = turn(sums_ref[0], all_cosine_ref[...], -all_sine_ref[...])
        out_ref[:, split : split + width] = turned.astype(low)
        out_ref[:, split + width :] = sums_ref[1].astype(low)


def attention_back(grad, queries, keys, values, places, cosine, sine, scale):
    length, width = keys.shape
    heads = queries.shape[1] // width
    tile = 256
    rows = lambda cols: pl.BlockSpec((tile, cols), lambda i: (i, 0))
    whole = lambda *shape: pl.BlockSpec(shape, lambda i: (0, 0))
    half = cosine.shape[1]
    return pl.pallas_call(
        functools.partial(attention_back_kernel, heads, scale),
        out_shape=jax.ShapeDtypeStruct((length, (heads + 2) * width), low),
        grid=(length // tile,),
        in_specs=[
            rows(heads * width),
            rows(heads * width),
            whole(length, width),
            whole(length, width),
            rows(1),
            whole(1, length),
            rows(half),
            rows(half),
            whole(length, half),
            whole(length, half),
        ],
        out_specs=whole(length, (heads + 2) * width),
        scratch_shapes=[pltpu.VMEM((2, length, width), wide)],
        compiler_params=pltpu.CompilerParams(vmem_limit_bytes=48 * 2**20),
        cost_estimate=pl.CostEstimate(
            flops=20 * heads * length * length * width,
            bytes_accessed=16 * length * width,
            transcendentals=2 * heads * length * length,
        ),
    )(
        grad,
        queries,
        keys,
        values,
        places[:, None],
        places[None, :],
        cosine,
        sine,
        cosine,
        sine,
    )


def column_tile(cols):
    return next(t for t in (256, 128, cols) if cols % t == 0)


def row_chunks(rows, body):
    size = next(t for t in (512, 256, 128, rows) if rows % t == 0)

    def step(i, carry):
        body(pl.ds(pl.multiple_of(i * size, size), size))
        return carry

    lax.fori_loop(0, rows // size, step, 0)


def units_kernel(x_ref, gate_ref, up_ref, hidden_ref, gate_slope_ref, up_slope_ref):
    root = (2.0 / jnp.pi) ** 0.5

    def body(at):
        x = x_ref[at, :]
        gate = dot(x, gate_ref[...])
        up = dot(x, up_ref[...])
        square = gate * gate
        bend = jnp.tanh(root * gate * (1.0 + 0.044715 * square))
        half = 0.5 * (1.0 + bend)
        activated = gate * half
        slope = half + 0.5 * gate * (1.0 - bend * bend) * root * (1.0 + 3.0 * 0.044715 * square)
        hidden_ref[at, :] = (activated * up).astype(low)
        gate_slope_ref[at, :] = (up * slope).astype(low)
        up_slope_ref[at, :] = activated.astype(low)

    row_chunks(x_ref.shape[0], body)


def units_forward(x, weights):
    rows, depth = x.shape
    cols = weights.shape[1] // 2
    tile = column_tile(cols)
    steps = cols // tile
    out = jax.ShapeDtypeStruct((rows, cols), low)
    out_spec = pl.BlockSpec((rows, tile), lambda j: (0, j))
    return pl.pallas_call(
        units_kernel,
        out_shape=[out] * 3,
        grid=(steps,),
        in_specs=[
            pl.BlockSpec((rows, depth), lambda j: (0, 0)),
            pl.BlockSpec((depth, tile), lambda j: (0, j)),
            pl.BlockSpec((depth, tile), lambda j: (0, j + steps)),
        ],
        out_specs=[out_spec] * 3,
        compiler_params=pltpu.CompilerParams(vmem_limit_bytes=48 * 2**20),
        cost_estimate=pl.CostEstimate(
            flops=4 * rows * depth * cols,
            bytes_accessed=4 * depth * cols + 2 * rows * depth + 6 * rows * cols,
            transcendentals=rows * cols,
        ),
    )(x, weights, weights)


def units_back_kernel(count, *refs):
    grads, weights = refs[:count], refs[count : 2 * count]
    gate_slope_ref, up_slope_ref, gate_ref, up_ref = refs[2 * count :]
    cols = gate_slope_ref.shape[1]
    tile = column_tile(cols)

    def step(j, carry):
        at = pl.ds(pl.multiple_of(j * tile, tile), tile)
        grad = sum(contract_last(g[...], w[at, :]) for g, w in zip(grads, weights))
        gate_ref[:, at] = (grad * gate_slope_ref[:, at].astype(wide)).astype(low)
        up_ref[:, at] = (grad * up_slope_ref[:, at].astype(wide)).astype(low)
        return carry

    lax.fori_loop(0, cols // tile, step, 0)


def units_back(grads, weights, gate_slope, up_slope):
    rows, cols = gate_slope.shape
    tile = next(t for t in (512, 256, 128, rows) if rows % t == 0)
    width = sum(g.shape[1] for g in grads)
    return pl.pallas_call(
        functools.partial(units_back_kernel, len(grads)),
        out_shape=[jax.ShapeDtypeStruct((rows, cols), low)] * 2,
        grid=(rows // tile,),
        in_specs=[pl.BlockSpec((tile, g.shape[1]), lambda i: (i, 0)) for g in grads]
        + [pl.BlockSpec(w.shape, lambda i: (0, 0)) for w in weights]
        + [pl.BlockSpec((tile, cols), lambda i: (i, 0))] * 2,
        out_specs=[pl.BlockSpec((tile, cols), lambda i: (i, 0))] * 2,
        compiler_params=pltpu.CompilerParams(vmem_limit_bytes=56 * 2**20),
        cost_estimate=pl.CostEstimate(
            flops=2 * rows * width * cols,
            bytes_accessed=2 * width * cols + 2 * rows * width + 8 * rows * cols,
            transcendentals=0,
        ),
    )(*grads, *weights, gate_slope, up_slope)


def product_kernel(*refs):
    *lefts, right_ref, out_ref = refs
    depth = lefts[0].shape[1]

    def body(at):
        total = sum(
            contract_last(left[at, :], right_ref[:, i * depth : (i + 1) * depth])
            for i, left in enumerate(lefts)
        )
        out_ref[at, :] = total.astype(out_ref.dtype)

    row_chunks(lefts[0].shape[0], body)


def product_last(lefts, right):
    rows, depth = lefts[0].shape
    cols, width = right.shape
    tile = column_tile(cols)
    return pl.pallas_call(
        product_kernel,
        out_shape=jax.ShapeDtypeStruct((rows, cols), low),
        grid=(cols // tile,),
        in_specs=[pl.BlockSpec((rows, depth), lambda j: (0, 0)) for _ in lefts]
        + [pl.BlockSpec((tile, width), lambda j: (j, 0))],
        out_specs=pl.BlockSpec((rows, tile), lambda j: (0, j)),
        compiler_params=pltpu.CompilerParams(vmem_limit_bytes=48 * 2**20),
        cost_estimate=pl.CostEstimate(
            flops=2 * rows * width * cols,
            bytes_accessed=2 * (rows * width + width * cols + rows * cols),
            transcendentals=0,
        ),
    )(*lefts, right)


def cores_apart_kernel(count, x_ref, out_ref):
    part = x_ref.shape[1] // count
    order = [*range(0, count, 2), *range(1, count, 2)]
    out_ref[...] = jnp.concatenate(
        [x_ref[:, b * part : (b + 1) * part] for b in order], axis=1
    )


def cores_apart(x, count):
    rows, cols = x.shape
    return pl.pallas_call(
        functools.partial(cores_apart_kernel, count),
        out_shape=jax.ShapeDtypeStruct(x.shape, x.dtype),
        grid=(rows // 128,),
        in_specs=[pl.BlockSpec((128, cols), lambda i: (i, 0))],
        out_specs=pl.BlockSpec((128, cols), lambda i: (i, 0)),
        compiler_params=pltpu.CompilerParams(vmem_limit_bytes=32 * 2**20),
        cost_estimate=pl.CostEstimate(
            flops=0, bytes_accessed=4 * rows * cols, transcendentals=0
        ),
    )(x)


def frequencies(half, head_dim):
    return rope_base ** (-(jnp.arange(half, dtype=wide) * 2.0) / head_dim)


def rotate(vectors, cosine, sine):
    half = vectors.shape[-1] // 2
    first = vectors[..., :half]
    second = vectors[..., half:]
    return jnp.concatenate(
        [first * cosine - second * sine, second * cosine + first * sine], axis=-1
    )


def inverse_rms(vectors):
    return lax.rsqrt(jnp.mean(vectors * vectors, axis=-1, keepdims=True) + epsilon)


def norm_back(vectors, inverse, gain, upstream):
    scaled = upstream * gain
    unit = vectors * inverse
    grad_vectors = inverse * (scaled - unit * jnp.mean(unit * scaled, axis=-1, keepdims=True))
    return (grad_vectors, jnp.sum(upstream * unit, axis=0))


def dot(left, right):
    return jnp.dot(left, right, preferred_element_type=wide)


def contract_last(left, right):
    return lax.dot_general(left, right, (((1,), (1,)), ((), ())), preferred_element_type=wide)


def contract_first(left, right):
    return lax.dot_general(left, right, (((0,), (0,)), ((), ())), preferred_element_type=wide)


def per_device(
    inputs,
    positions,
    pre_attn_gain,
    post_attn_gain,
    pre_mlp_gain,
    post_mlp_gain,
    query_weight,
    key_weight,
    value_weight,
    out_weight,
    gate_weight,
    up_weight,
    down_weight,
    cotangent,
):
    n_ctx, n_fsdp = lax.axis_size("ctx"), lax.axis_size("fsdp")
    c, f = lax.axis_index("ctx"), lax.axis_index("fsdp")
    rows = inputs[0].astype(wide)
    tokens, width = rows.shape
    length = n_ctx * tokens
    scale = HD ** (-0.5)
    my_heads = HQ // n_ctx
    my_kv = max(KV // n_ctx, 1)
    share = max(n_ctx // KV, 1)
    groups = my_heads // my_kv
    kv_start = (c // share) * my_kv * HD
    query_cols, kv_cols = my_heads * HD, my_kv * HD
    out_cols = width // n_ctx
    ff_rows = down_weight.shape[0]
    part = ff_rows // n_ctx
    main = ff_rows // 128 // n_ctx * 128
    rest = part - main
    chips = n_fsdp // 2
    tiled = ff_rows % 128 == 0 and main > 0 and rest * n_ctx == 128 and rest % 16 == 0
    tiled = tiled and chips * rest % 128 == 0 and query_cols % 256 == 0
    last_cols = width // 384 * 128

    def gathered(shard):
        return lax.all_gather(shard, "fsdp", axis=0, tiled=True)

    def units_together(full):
        if not tiled:
            return full
        moves = []
        for block in range(n_fsdp):
            to = unit_place(block, n_fsdp, main, rest)
            moves.append((block * part, main, to, 0))
            to = rest_place(block % 2, n_fsdp, main, rest) + block // 2 * rest
            moves.append((block * part + main, rest, to, 0))
        return place([(full, 0, moves)], jnp.zeros((), jnp.int32), full.shape, 0, full.dtype)

    def chip_term(term):
        return chip_sum(term.astype(low))

    def unit_term(left, right):
        if not tiled:
            return chip_term(contract_first(left, right))
        half, core = chips * part, f & 1
        theirs = lax.dynamic_slice_in_dim(left, (1 - core) * half, half, 1)
        theirs = swap(contract_first(theirs, right).astype(low), "fsdp", 1)
        mine = contract_first(lax.dynamic_slice_in_dim(left, core * half, half, 1), right)
        moves = [(chip * main, main, chip * part) for chip in range(chips)]
        moves += [
            (chips * main + chip * rest, rest, chip * part + main) for chip in range(chips)
        ]
        return add_rows(mine.astype(low), theirs, moves)

    def weight_term(left, right):
        if not tiled:
            return chip_term(contract_first(left, right))
        half, core = left.shape[1] // 2, f & 1
        theirs = lax.dynamic_slice_in_dim(left, (1 - core) * half, half, 1)
        theirs = swap(contract_first(theirs, right).astype(low), "fsdp", 1)
        mine = contract_first(lax.dynamic_slice_in_dim(left, core * half, half, 1), right)
        return (mine + theirs.astype(wide)).astype(low)

    def my_units(weight):
        if tiled:
            return take_units(weight, c, n_fsdp, main, rest)
        split = weight.reshape(weight.shape[0], n_fsdp, n_ctx, part)
        return lax.dynamic_index_in_dim(split, c, 2, keepdims=False).reshape(
            weight.shape[0], n_fsdp * part
        )

    def in_order(blocks):
        blocks = list(blocks)
        for bit in range(n_ctx.bit_length() - 1):
            mask = 1 << bit
            odd = (c & mask) != 0
            blocks = [jnp.where(odd, blocks[k ^ mask], blocks[k]) for k in range(n_ctx)]
        return blocks

    def token_blocks(array):
        return [array[k * tokens : (k + 1) * tokens] for k in range(n_ctx)]

    def block_order(blocks, k):
        pieces = blocks.reshape(n_ctx, tokens, blocks.shape[-1])
        return jnp.concatenate([pieces[k ^ m] for m in range(n_ctx)], axis=0)

    def from_columns(array):
        got = jnp.stack(exchange(token_blocks(array)))
        return jnp.transpose(jnp.take(got, jnp.arange(n_ctx) ^ c, axis=0), (1, 0, 2)).reshape(
            tokens, width
        )

    def to_columns(array):
        split = array.reshape(tokens, n_ctx, out_cols)
        split = jnp.take(split, jnp.arange(n_ctx) ^ c, axis=1)
        return jnp.concatenate(exchange([split[:, k] for k in range(n_ctx)]), axis=0)

    my_qkv = jnp.concatenate(
        [
            lax.dynamic_slice_in_dim(query_weight, c * query_cols, query_cols, 1),
            lax.dynamic_slice_in_dim(key_weight, kv_start, kv_cols, 1),
            lax.dynamic_slice_in_dim(value_weight, kv_start, kv_cols, 1),
        ],
        axis=1,
    )
    full_qkv = gathered(my_qkv)
    full_out = gathered(lax.dynamic_slice_in_dim(out_weight, c * out_cols, out_cols, 1))
    full_units = gathered(jnp.concatenate([my_units(gate_weight), my_units(up_weight)], axis=1))
    if tiled:
        my_down = jnp.concatenate(
            [
                lax.dynamic_slice_in_dim(down_weight, c * main, main, 0),
                lax.dynamic_slice_in_dim(down_weight, n_ctx * main + c * rest, rest, 0),
            ],
            axis=0,
        )
    else:
        my_down = lax.dynamic_slice_in_dim(down_weight, c * part, part, 0)
    gains = jnp.stack([pre_attn_gain, post_attn_gain, pre_mlp_gain, post_mlp_gain])
    gains = jnp.stack([gains if k == 0 else swap(gains, "fsdp", k) for k in range(n_fsdp)])
    gains = jnp.take(gains, jnp.arange(n_fsdp) ^ f, axis=0)
    gains = jnp.transpose(gains, (1, 0, 2)).reshape(4, width).astype(wide)
    gain_a, gain_b, gain_c, gain_d = gains[0], gains[1], gains[2], gains[3]

    inverse_a = inverse_rms(rows)
    normed = join(gather_pieces((rows * inverse_a * gain_a).astype(low)))
    places = jnp.concatenate(gather_blocks(positions[0], halves=False), axis=0)
    angles = places.astype(wide)[:, None] * frequencies(HD // 2, HD)
    cosine, sine = jnp.cos(angles), jnp.sin(angles)
    projected = dot(normed, full_qkv)
    query_lin = projected[:, :query_cols].reshape(length, my_heads, HD)
    key_lin = projected[:, query_cols : query_cols + kv_cols].reshape(length, my_kv, HD)
    values = projected[:, query_cols + kv_cols :].astype(low).reshape(length, my_kv, HD)
    queries = (rotate(query_lin, cosine[:, None], sine[:, None]) * scale).astype(low)
    keys = rotate(key_lin, cosine[:, None], sine[:, None]).astype(low)
    queries = queries.reshape(length, my_kv, groups, HD)
    allowed = places[None, :] <= places[:, None]
    raw = jnp.einsum("tkgd,rkd->kgtr", queries, keys, preferred_element_type=wide)
    bent = jnp.tanh(raw / soft_cap)
    weights = jnp.where(allowed, jnp.exp(soft_cap * bent), 0.0)
    total = jnp.sum(weights, axis=-1)
    mixed = jnp.einsum("kgtr,rkd->kgtd", weights.astype(low), values, preferred_element_type=wide)
    mixed = mixed / total[..., None]
    attn = jnp.transpose(mixed, (2, 0, 1, 3)).reshape(length, query_cols).astype(low)

    if tiled:
        pieces = [
            (array, k, [(0, array.shape[1], first, query_cols)])
            for array, k, first in gather_pieces(attn)
        ]
        attn_all = place(pieces, c, (length, HQ * HD), 1, low, blocks=n_ctx)
    else:
        attn_blocks = [block_order(block, k) for k, block in enumerate(gather_blocks(attn))]
        attn_all = jnp.concatenate(in_order(attn_blocks), axis=1)
    branch = from_columns(dot(attn_all, full_out).astype(low)).astype(wide)
    inverse_b = inverse_rms(branch)
    middle = rows + branch * inverse_b * gain_b
    inverse_c = inverse_rms(middle)

    normed_mlp = join(gather_pieces((middle * inverse_c * gain_c).astype(low)))
    normed_mlp_apart = cores_apart(normed_mlp, n_fsdp) if tiled else normed_mlp
    my_down = after(my_down, full_units, normed_mlp_apart)
    first_down, last_down = gathered(my_down[:, :-last_cols]), my_down[:, -last_cols:]
    hidden, gate_slope, up_slope = units_forward(normed_mlp, full_units)
    last_down = gathered(after(last_down, first_down, hidden))
    full_downs = [units_together(first_down), units_together(last_down)]
    first_terms, last_terms = (
        token_blocks(dot(hidden, full).astype(low)) for full in full_downs
    )
    last_terms = sum(term.astype(wide) for term in exchange(last_terms))
    down = jnp.concatenate([scatter_sum(halved(first_terms)), last_terms], axis=1)
    inverse_d = inverse_rms(down)
    output = (middle + down * inverse_d * gain_d).astype(low)[None]

    grad_result = cotangent[0].astype(wide)
    grad_down, grad_gain_d = norm_back(down, inverse_d, gain_d, grad_result)
    grad_down = grad_down.astype(low)
    pieces = gather_pieces(grad_down[:, -last_cols:])
    grad_downs = [join(pieces)]
    down_terms = [unit_term(hidden, grad_downs[0])]
    others = [array for array, _, _ in pieces[1:3]]
    pieces = gather_pieces(after(grad_down[:, :-last_cols], *others))
    pieces[0] = (after(pieces[0][0], down_terms[0]), *pieces[0][1:])
    grad_downs.append(join(pieces))
    down_terms.append(unit_term(hidden, grad_downs[1]))
    grad_downs, down_terms[1] = lax.optimization_barrier((grad_downs, down_terms[1]))
    down_sums = [fsdp_sum(term) for term in down_terms]
    grad_gate, grad_up = units_back(grad_downs, full_downs[::-1], gate_slope, up_slope)
    grad_normed_mlp = product_last([grad_gate, grad_up], full_units)
    grad_normed_mlp, grad_gate = lax.optimization_barrier((grad_normed_mlp, grad_gate))
    gate_term = weight_term(normed_mlp_apart, after(grad_gate, down_sums[0]))
    gate_sum = fsdp_sum(gate_term)
    up_term = weight_term(normed_mlp_apart, after(grad_up, gate_term))
    up_sum = fsdp_sum(up_term)
    grad_normed_mlp = scatter_sum(halved(token_blocks(grad_normed_mlp)))
    down_pieces = [gather_pieces(after(down_sums[0], grad_gate))]
    arrived = [piece[0] for piece in down_pieces[0]]
    grad_normed_mlp = after(grad_normed_mlp, up_term, down_sums[1], *arrived)
    down_pieces.append(gather_pieces(after(down_sums[1], grad_normed_mlp)))
    grad_middle_mlp, grad_gain_c = norm_back(middle, inverse_c, gain_c, grad_normed_mlp)
    grad_middle = grad_result + grad_middle_mlp
    grad_branch, grad_gain_b = norm_back(branch, inverse_b, gain_b, grad_middle)

    arrived = [piece[0] for piece in down_pieces[1][1:3]]
    grad_branch_cols = to_columns(after(grad_branch.astype(low), *arrived))
    out_term = contract_first(attn_all, grad_branch_cols).astype(low)
    grad_attn_all = contract_last(grad_branch_cols, full_out).astype(low)
    if tiled:
        parts = split_columns(grad_attn_all, c, n_ctx, cut_at(query_cols))
        grad_attn = scatter_sum(list(zip(parts[::2], parts[1::2]))).astype(low)
    else:
        parts = [
            lax.dynamic_slice_in_dim(grad_attn_all, (c ^ k) * query_cols, query_cols, 1)
            for k in range(n_ctx)
        ]
        parts = [block_order(part_, k) for k, part_ in enumerate(parts)]
        grad_attn = scatter_sum(halved(parts)).astype(low)
    grad_attn = after(grad_attn, gate_sum, *[piece[0] for piece in down_pieces[1]])
    gate_pieces = gather_pieces(after(gate_sum, grad_attn))
    grad_projected = attention_back(
        grad_attn,
        queries.reshape(length, query_cols),
        keys.reshape(length, kv_cols),
        values.reshape(length, kv_cols),
        places,
        cosine,
        sine,
        scale,
    )
    grad_projected = after(grad_projected, *[piece[0] for piece in gate_pieces[1:3]])
    qkv_term = contract_first(normed, grad_projected).astype(low)
    pad = (qkv_term.shape[0] - out_term.shape[0]) // n_fsdp
    out_term = jnp.pad(out_term.reshape(n_fsdp, -1, out_cols), ((0, 0), (0, pad), (0, 0)))
    out_term = out_term.reshape(qkv_term.shape[0], out_cols)
    attn_sum = lax.psum_scatter(
        jnp.concatenate([qkv_term, out_term], axis=1), "fsdp", scatter_dimension=0, tiled=True
    )
    qkv_sum = attn_sum[:, : qkv_term.shape[1]]
    out_sum = attn_sum[: attn_sum.shape[0] - pad, qkv_term.shape[1] :]
    grad_normed = contract_last(grad_projected, full_qkv).astype(low)
    grad_normed = scatter_sum(halved(token_blocks(grad_normed)))
    grad_normed = after(grad_normed, up_sum)
    grad_rows, grad_gain_a = norm_back(rows, inverse_a, gain_a, grad_normed)
    input_grad = (grad_middle + grad_rows).astype(low)[None]

    gain_terms = jnp.stack([grad_gain_a, grad_gain_b, grad_gain_c, grad_gain_d])
    for bit in range(n_ctx.bit_length() - 1):
        gain_terms = gain_terms + swap(gain_terms, "ctx", 1 << bit)
    gain_terms = jnp.transpose(gain_terms.reshape(4, n_fsdp, width // n_fsdp), (1, 0, 2))
    gain_terms = jnp.take(gain_terms, jnp.arange(n_fsdp) ^ f, axis=0)
    gain_sums = gain_terms[0]
    for k in range(1, n_fsdp):
        gain_sums = gain_sums + swap(gain_terms[k], "fsdp", k)

    if share == 1:
        qkv_pieces = gather_pieces(qkv_sum)

        def columns_of(first, size, shape):
            pieces = []
            for array, k, start in qkv_pieces:
                begin, end = max(first, start), min(first + size, start + array.shape[1])
                if begin < end:
                    pieces.append((array, k, [(begin - start, size, 0, size)]))
            return place(pieces, c, shape, 1, wide)

        query_grad = columns_of(0, query_cols, query_weight.shape)
        key_grad = columns_of(query_cols, kv_cols, key_weight.shape)
        value_grad = columns_of(query_cols + kv_cols, kv_cols, value_weight.shape)
    else:
        qkv_blocks = gather_blocks(qkv_sum)
        query_grad = jnp.zeros(query_weight.shape, wide)
        key_grad = jnp.zeros(key_weight.shape, wide)
        value_grad = jnp.zeros(value_weight.shape, wide)
        for k, block in enumerate(qkv_blocks):
            query_grad = lax.dynamic_update_slice_in_dim(
                query_grad, block[:, :query_cols].astype(wide), (c ^ k) * query_cols, 1
            )
        for k in range(0, n_ctx, share):
            block = sum(qkv_blocks[k + s][:, query_cols:].astype(wide) for s in range(share))
            start = ((c ^ k) // share) * kv_cols
            key_grad = lax.dynamic_update_slice_in_dim(key_grad, block[:, :kv_cols], start, 1)
            value_grad = lax.dynamic_update_slice_in_dim(value_grad, block[:, kv_cols:], start, 1)

    out_grad = jnp.concatenate(in_order(gather_blocks(out_sum)), axis=1).astype(wide)

    def all_units(gathered_pieces):
        if not tiled:
            blocks = as_blocks(gathered_pieces)
            blocks = [b.reshape(b.shape[0], n_fsdp, part) for b in in_order(blocks)]
            return jnp.stack(blocks, axis=2).reshape(gate_weight.shape).astype(wide)
        pieces, tails = [], []
        for array, k, start in gathered_pieces:
            moves = []
            for b in range(n_fsdp):
                begin = unit_place(b, n_fsdp, main, rest) - start
                if 0 <= begin < array.shape[1]:
                    moves.append((begin, main, b * ff_rows, main))
            pieces.append((array, k, moves))
            for core in (0, 1):
                begin = rest_place(core, n_fsdp, main, rest) - start
                if 0 <= begin < array.shape[1]:
                    tails.append((k, core, array[:, begin : begin + chips * rest]))
        tails = [tail for _, _, tail in sorted(tails, key=lambda item: item[:2])]
        source = jnp.arange(n_ctx * n_fsdp * rest)[:, None]
        index, unit = source // (n_fsdp * rest), source % (n_fsdp * rest)
        block = unit // rest % chips * 2 + unit // (chips * rest)
        target = block * 128 + (c ^ index) * rest + unit % rest
        spread_to = (target == jnp.arange(n_fsdp * 128)[None, :]).astype(low)
        return place(
            pieces,
            c,
            gate_weight.shape,
            1,
            wide,
            dot(jnp.concatenate(tails, axis=1), spread_to),
            [(b * 128, 128, (b + 1) * ff_rows - 128) for b in range(n_fsdp)],
        )

    gate_arrays = lax.optimization_barrier(([piece[0] for piece in gate_pieces], qkv_term))[0]
    gate_grad = all_units([(a, *piece[1:]) for a, piece in zip(gate_arrays, gate_pieces)])
    up_grad = all_units(gather_pieces(up_sum))
    down_halves = zip(*[as_blocks(pieces) for pieces in down_pieces[::-1]])
    down_blocks = [jnp.concatenate(block, axis=1) for block in down_halves]
    down_blocks[0] = after(down_blocks[0], qkv_term)
    if tiled:
        moves = [(0, main, 0, main), (main, rest, n_ctx * main, rest)]
        pieces = [(block, k, moves) for k, block in enumerate(down_blocks)]
        down_grad = place(pieces, c, down_weight.shape, 0, wide)
    else:
        down_grad = jnp.concatenate(in_order(down_blocks), axis=0).astype(wide)
    return (
        output,
        input_grad,
        gain_sums[0],
        gain_sums[1],
        gain_sums[2],
        gain_sums[3],
        query_grad,
        key_grad,
        value_grad,
        out_grad,
        gate_grad,
        up_grad,
        down_grad,
    )


def solution(mesh):
    return jax.shard_map(
        per_device,
        mesh=mesh,
        in_specs=(
            P("fsdp", "ctx", None),
            P("fsdp", "ctx"),
            P("fsdp"),
            P("fsdp"),
            P("fsdp"),
            P("fsdp"),
            P("fsdp", None),
            P("fsdp", None),
            P("fsdp", None),
            P("fsdp", None),
            P("fsdp", None),
            P("fsdp", None),
            P("fsdp", None),
            P("fsdp", "ctx", None),
        ),
        out_specs=(
            P("fsdp", "ctx", None),
            P("fsdp", "ctx", None),
            P("fsdp"),
            P("fsdp"),
            P("fsdp"),
            P("fsdp"),
            P("fsdp", None),
            P("fsdp", None),
            P("fsdp", None),
            P("fsdp", None),
            P("fsdp", None),
            P("fsdp", None),
            P("fsdp", None),
        ),
        check_vma=False,
    )
```

```python
import functools

import jax
import jax.numpy as jnp
from jax import lax
from jax.experimental import pallas as pl
from jax.experimental.pallas import tpu as pltpu
from jax.sharding import PartitionSpec as P

HQ = 8
KV = 4
HD = 256

soft_cap = 50.0
epsilon = 1e-06
rope_base = 10000.0
low = jnp.bfloat16
wide = jnp.float32


def swap(shard, axis, mask):
    size = lax.axis_size(axis)
    return lax.ppermute(shard, axis, [(i, i ^ mask) for i in range(size)])


def after(value, *others):
    return lax.optimization_barrier((value, *others))[0]


def chip_groups():
    size = lax.axis_size("fsdp")
    return [list(range(core, size, 2)) for core in (0, 1)]


def cut_at(width):
    return (width // 512) * 256 if width >= 512 else width // 2


def gather_pieces(block, halves=True):
    width = block.shape[-1]
    got, pieces = {0: block}, [(block, 0, 0)]
    for k in range(1, lax.axis_size("ctx")):
        low_bit, high_bit = k & -k, 1 << (k.bit_length() - 1)
        if low_bit == high_bit or not halves:
            got[k] = swap(got[k ^ high_bit], "ctx", high_bit)
            pieces.append((got[k], k, 0))
        else:
            cut = cut_at(width)
            first = swap(got[k ^ high_bit][..., :cut], "ctx", high_bit)
            second = swap(got[k ^ low_bit][..., cut:], "ctx", low_bit)
            pieces += [(first, k, 0), (second, k, cut)]
            if k + 1 < lax.axis_size("ctx"):
                got[k] = jnp.concatenate([first, second], axis=-1)
    return pieces


def gather_blocks(block, halves=True):
    return as_blocks(gather_pieces(block, halves))


def as_blocks(pieces):
    blocks = [[] for _ in range(lax.axis_size("ctx"))]
    for array, k, _ in pieces:
        blocks[k].append(array)
    return [b[0] if len(b) == 1 else jnp.concatenate(b, axis=-1) for b in blocks]


def halved(parts):
    cut = cut_at(parts[0].shape[-1])
    return [(part[..., :cut], part[..., cut:]) for part in parts]


def scatter_sum(terms):
    terms = list(terms)
    for k in range(len(terms) - 1, 0, -1):
        low_bit, high_bit = k & -k, 1 << (k.bit_length() - 1)
        first = swap(terms[k][0], "ctx", high_bit).astype(wide)
        second = swap(terms[k][1], "ctx", low_bit).astype(wide)
        to_first, to_second = k ^ high_bit, k ^ low_bit
        first = terms[to_first][0].astype(wide) + first
        terms[to_first] = (first.astype(low) if to_first else first, terms[to_first][1])
        second = terms[to_second][1].astype(wide) + second
        terms[to_second] = (terms[to_second][0], second.astype(low) if to_second else second)
    return jnp.concatenate(terms[0], axis=-1)


def exchange(parts):
    return [parts[0]] + [swap(part, "ctx", k) for k, part in enumerate(parts) if k]


def chip_sum(term):
    count = lax.axis_size("fsdp")
    core = lax.axis_index("fsdp") & 1
    halves = term.reshape(count // 2, 2, term.shape[0] // count, term.shape[1])
    theirs = swap(lax.dynamic_index_in_dim(halves, 1 - core, 1, keepdims=False), "fsdp", 1)
    mine = lax.dynamic_index_in_dim(halves, core, 1, keepdims=False)
    total = (mine.astype(wide) + theirs.astype(wide)).astype(low)
    return total.reshape(-1, term.shape[1])


def fsdp_sum(arr):
    return lax.psum_scatter(
        arr,
        "fsdp",
        scatter_dimension=0,
        tiled=True,
        axis_index_groups=chip_groups(),
    )


def row_tile(rows):
    return next(t for t in (48, 32, 16, rows) if rows % t == 0)


def unit_place(block, count, main, rest):
    return block % 2 * (count // 2) * (main + rest) + block // 2 * main


def rest_place(core, count, main, rest):
    return core * (count // 2) * (main + rest) + count // 2 * main


def take_units_kernel(count, cols, main, rest, c_ref, weight_ref, pick_ref, out_ref):
    c = c_ref[0]
    for b in range(count):
        start = pl.multiple_of(b * cols + c * main, 128)
        to = unit_place(b, count, main, rest)
        out_ref[:, to : to + main] = weight_ref[:, pl.ds(start, main)]
    last = jnp.concatenate(
        [weight_ref[:, (b + 1) * cols - 128 : (b + 1) * cols] for b in range(count)], axis=1
    )
    picked = jnp.dot(last, pick_ref[...], preferred_element_type=jnp.float32)
    size = count // 2 * rest
    for core in (0, 1):
        to = rest_place(core, count, main, rest)
        out_ref[:, to : to + size] = picked[:, core * size : (core + 1) * size].astype(out_ref.dtype)


def take_units(weight, c, count, main, rest):
    rows, cols = weight.shape
    source = jnp.arange(count * 128)[:, None]
    target = jnp.arange(count * rest)[None, :]
    block = target // rest % (count // 2) * 2 + target // (count // 2 * rest)
    pick = (source == block * 128 + c * rest + target % rest).astype(weight.dtype)
    tile = row_tile(rows)
    return pl.pallas_call(
        functools.partial(take_units_kernel, count, cols // count, main, rest),
        out_shape=jax.ShapeDtypeStruct((rows, count * (main + rest)), weight.dtype),
        grid=(rows // tile,),
        in_specs=[
            pl.BlockSpec(memory_space=pltpu.SMEM),
            pl.BlockSpec((tile, cols), lambda i: (i, 0)),
            pl.BlockSpec(pick.shape, lambda i: (0, 0)),
        ],
        out_specs=pl.BlockSpec((tile, count * (main + rest)), lambda i: (i, 0)),
        compiler_params=pltpu.CompilerParams(vmem_limit_bytes=32 * 2**20),
        cost_estimate=pl.CostEstimate(
            flops=2 * rows * count * 128 * count * rest,
            bytes_accessed=3 * rows * cols,
            transcendentals=0,
        ),
    )(c.reshape(1), weight, pick)


def place_kernel(plan, fixed, axis, i_ref, *refs):
    out = refs[-1]
    index = i_ref[0]
    for ref, (k, moves) in zip(refs, plan):
        for start, size, base, stride in moves:
            to = base + (index ^ k) * stride
            if stride:
                to = pl.multiple_of(to, 16 if axis == 0 else 128)
            if axis == 0:
                out[pl.ds(to, size), :] = ref[start : start + size, :].astype(out.dtype)
            else:
                out[:, pl.ds(to, size)] = ref[:, start : start + size].astype(out.dtype)
    for start, size, base in fixed:
        out[:, base : base + size] = refs[len(plan)][:, start : start + size]


def place(pieces, index, shape, axis, dtype, extra=None, fixed=(), blocks=0):
    arrays = [array for array, _, _ in pieces]
    plan = [(k, moves) for _, k, moves in pieces]
    if axis == 1:
        tile = shape[0] // blocks if blocks else row_tile(shape[0])
        grid = shape[0] // tile
        block = lambda array: (tile, array.shape[1])
        at = lambda i: (i, 0)
        out_block = (tile, shape[1])
    else:
        tile = next(t for t in (384, 256, 128, shape[1]) if shape[1] % t == 0)
        grid = shape[1] // tile
        block = lambda array: (array.shape[0], tile)
        at = lambda i: (0, i)
        out_block = (shape[0], tile)
    ats = [at] * len(plan)
    if blocks:
        ats = [lambda i, k=k: (i ^ k, 0) for k, _ in plan]
    if extra is not None:
        arrays.append(extra)
        ats.append(at)
    return pl.pallas_call(
        functools.partial(place_kernel, plan, fixed, axis),
        out_shape=jax.ShapeDtypeStruct(shape, dtype),
        grid=(grid,),
        in_specs=[pl.BlockSpec(memory_space=pltpu.SMEM)]
        + [pl.BlockSpec(block(array), place_) for array, place_ in zip(arrays, ats)],
        out_specs=pl.BlockSpec(out_block, at),
        compiler_params=pltpu.CompilerParams(vmem_limit_bytes=32 * 2**20),
        cost_estimate=pl.CostEstimate(
            flops=0, bytes_accessed=6 * shape[0] * shape[1], transcendentals=0
        ),
    )(index.reshape(1), *arrays)


def add_rows_kernel(moves, first_ref, second_ref, out_ref):
    for start, size, to in moves:
        total = first_ref[start : start + size, :].astype(wide)
        total += second_ref[start : start + size, :].astype(wide)
        out_ref[to : to + size, :] = total.astype(out_ref.dtype)


def add_rows(first, second, moves):
    rows, cols = first.shape
    tile = next(t for t in (384, 256, 128) if cols % t == 0)
    spec = pl.BlockSpec((rows, tile), lambda i: (0, i))
    return pl.pallas_call(
        functools.partial(add_rows_kernel, moves),
        out_shape=jax.ShapeDtypeStruct((rows, cols), first.dtype),
        grid=(cols // tile,),
        in_specs=[spec, spec],
        out_specs=spec,
        compiler_params=pltpu.CompilerParams(vmem_limit_bytes=32 * 2**20),
        cost_estimate=pl.CostEstimate(
            flops=rows * cols, bytes_accessed=6 * rows * cols, transcendentals=0
        ),
    )(first, second)


def split_columns_kernel(size, cut, c_ref, ref, *outs):
    c = c_ref[0]
    for k in range(len(outs) // 2):
        start = pl.multiple_of((c ^ k) * size, 128)
        outs[2 * k][...] = ref[:, pl.ds(start, cut)]
        outs[2 * k + 1][...] = ref[:, pl.ds(start + cut, size - cut)]


def split_columns(array, c, count, cut):
    rows, cols = array.shape
    tile, size = rows // count, cols // count
    shapes = [(rows, cut), (rows, size - cut)] * count
    return pl.pallas_call(
        functools.partial(split_columns_kernel, size, cut),
        out_shape=[jax.ShapeDtypeStruct(shape, array.dtype) for shape in shapes],
        grid=(count,),
        in_specs=[
            pl.BlockSpec(memory_space=pltpu.SMEM),
            pl.BlockSpec((tile, cols), lambda i: (i, 0)),
        ],
        out_specs=[
            pl.BlockSpec((tile, shape[1]), lambda i, k=n // 2: (i ^ k, 0))
            for n, shape in enumerate(shapes)
        ],
        compiler_params=pltpu.CompilerParams(vmem_limit_bytes=32 * 2**20),
        cost_estimate=pl.CostEstimate(
            flops=0, bytes_accessed=4 * rows * cols, transcendentals=0
        ),
    )(c.reshape(1), array)


def join_kernel(plan, *refs):
    out = refs[-1]
    for ref, (k, first) in zip(refs, plan):
        out[k, :, first : first + ref.shape[1]] = ref[...]


def join(pieces):
    rows, width = pieces[0][0].shape
    count = 1 + max(k for _, k, _ in pieces)
    if any(array.shape[1] % 128 for array, _, _ in pieces) or rows % 64:
        blocks = [[] for _ in range(count)]
        for array, k, _ in pieces:
            blocks[k].append(array)
        return jnp.concatenate([jnp.concatenate(b, axis=1) for b in blocks], axis=0)
    joined = pl.pallas_call(
        functools.partial(join_kernel, [(k, first) for _, k, first in pieces]),
        out_shape=jax.ShapeDtypeStruct((count, rows, width), pieces[0][0].dtype),
        grid=(rows // 64,),
        in_specs=[pl.BlockSpec((64, array.shape[1]), lambda i: (i, 0)) for array, _, _ in pieces],
        out_specs=pl.BlockSpec((count, 64, width), lambda i: (0, i, 0)),
        compiler_params=pltpu.CompilerParams(vmem_limit_bytes=32 * 2**20),
        cost_estimate=pl.CostEstimate(
            flops=0, bytes_accessed=4 * count * rows * width, transcendentals=0
        ),
    )(*[array for array, _, _ in pieces])
    return joined.reshape(count * rows, width)


def turn(vectors, cosine, sine):
    half = cosine.shape[1]
    parts = []
    for start in range(0, vectors.shape[1], 2 * half):
        first = vectors[:, start : start + half]
        second = vectors[:, start + half : start + 2 * half]
        parts += [first * cosine - second * sine, second * cosine + first * sine]
    return jnp.concatenate(parts, axis=1)


def attention_back_kernel(
    heads, scale, grad_ref, query_ref, key_ref, value_ref, row_ref, column_ref,
    cosine_ref, sine_ref, all_cosine_ref, all_sine_ref, out_ref, sums_ref,
):
    step = pl.program_id(0)
    keys, values = key_ref[...], value_ref[...]
    width = keys.shape[1]

    @pl.when(step == 0)
    def _():
        sums_ref[...] = jnp.zeros_like(sums_ref)

    allowed = column_ref[...] <= row_ref[...]
    grads = []
    for head in range(heads):
        at = slice(head * width, (head + 1) * width)
        query, grad = query_ref[:, at], grad_ref[:, at]
        bent = jnp.tanh(contract_last(query, keys) * (1.0 / soft_cap))
        weights = jnp.where(allowed, jnp.exp(soft_cap * bent), 0.0)
        probs = weights * (1.0 / jnp.sum(weights, axis=1, keepdims=True))
        grad_probs = contract_last(grad, values)
        delta = jnp.sum(probs * grad_probs, axis=1, keepdims=True)
        grad_raw = (probs * (grad_probs - delta) * (1.0 - bent * bent)).astype(low)
        grads.append(dot(grad_raw, keys))
        sums_ref[0] += contract_first(grad_raw, query)
        sums_ref[1] += contract_first(probs.astype(low), grad)
    grads = jnp.concatenate(grads, axis=1) * scale
    here = pl.ds(pl.multiple_of(step * grads.shape[0], grads.shape[0]), grads.shape[0])
    split = grads.shape[1]
    out_ref[here, :split] = turn(grads, cosine_ref[...], -sine_ref[...]).astype(low)

    @pl.when(step == pl.num_programs(0) - 1)
    def _():
        turned = turn(sums_ref[0], all_cosine_ref[...], -all_sine_ref[...])
        out_ref[:, split : split + width] = turned.astype(low)
        out_ref[:, split + width :] = sums_ref[1].astype(low)


def attention_back(grad, queries, keys, values, places, cosine, sine, scale):
    length, width = keys.shape
    heads = queries.shape[1] // width
    tile = 256
    rows = lambda cols: pl.BlockSpec((tile, cols), lambda i: (i, 0))
    whole = lambda *shape: pl.BlockSpec(shape, lambda i: (0, 0))
    half = cosine.shape[1]
    return pl.pallas_call(
        functools.partial(attention_back_kernel, heads, scale),
        out_shape=jax.ShapeDtypeStruct((length, (heads + 2) * width), low),
        grid=(length // tile,),
        in_specs=[
            rows(heads * width),
            rows(heads * width),
            whole(length, width),
            whole(length, width),
            rows(1),
            whole(1, length),
            rows(half),
            rows(half),
            whole(length, half),
            whole(length, half),
        ],
        out_specs=whole(length, (heads + 2) * width),
        scratch_shapes=[pltpu.VMEM((2, length, width), wide)],
        compiler_params=pltpu.CompilerParams(vmem_limit_bytes=48 * 2**20),
        cost_estimate=pl.CostEstimate(
            flops=20 * heads * length * length * width,
            bytes_accessed=16 * length * width,
            transcendentals=2 * heads * length * length,
        ),
    )(
        grad,
        queries,
        keys,
        values,
        places[:, None],
        places[None, :],
        cosine,
        sine,
        cosine,
        sine,
    )


def column_tile(cols):
    return next(t for t in (256, 128, cols) if cols % t == 0)


def row_chunks(rows, body):
    size = next(t for t in (512, 256, 128, rows) if rows % t == 0)

    def step(i, carry):
        body(pl.ds(pl.multiple_of(i * size, size), size))
        return carry

    lax.fori_loop(0, rows // size, step, 0)


def units_kernel(x_ref, gate_ref, up_ref, hidden_ref, gate_slope_ref, up_slope_ref):
    root = (2.0 / jnp.pi) ** 0.5

    def body(at):
        x = x_ref[at, :]
        gate = dot(x, gate_ref[...])
        up = dot(x, up_ref[...])
        square = gate * gate
        bend = jnp.tanh(root * gate * (1.0 + 0.044715 * square))
        half = 0.5 * (1.0 + bend)
        activated = gate * half
        slope = half + 0.5 * gate * (1.0 - bend * bend) * root * (1.0 + 3.0 * 0.044715 * square)
        hidden_ref[at, :] = (activated * up).astype(low)
        gate_slope_ref[at, :] = (up * slope).astype(low)
        up_slope_ref[at, :] = activated.astype(low)

    row_chunks(x_ref.shape[0], body)


def units_forward(x, weights):
    rows, depth = x.shape
    cols = weights.shape[1] // 2
    tile = column_tile(cols)
    steps = cols // tile
    out = jax.ShapeDtypeStruct((rows, cols), low)
    out_spec = pl.BlockSpec((rows, tile), lambda j: (0, j))
    return pl.pallas_call(
        units_kernel,
        out_shape=[out] * 3,
        grid=(steps,),
        in_specs=[
            pl.BlockSpec((rows, depth), lambda j: (0, 0)),
            pl.BlockSpec((depth, tile), lambda j: (0, j)),
            pl.BlockSpec((depth, tile), lambda j: (0, j + steps)),
        ],
        out_specs=[out_spec] * 3,
        compiler_params=pltpu.CompilerParams(vmem_limit_bytes=48 * 2**20),
        cost_estimate=pl.CostEstimate(
            flops=4 * rows * depth * cols,
            bytes_accessed=4 * depth * cols + 2 * rows * depth + 6 * rows * cols,
            transcendentals=rows * cols,
        ),
    )(x, weights, weights)


def units_back_kernel(count, *refs):
    grads, weights = refs[:count], refs[count : 2 * count]
    gate_slope_ref, up_slope_ref, gate_ref, up_ref = refs[2 * count :]
    cols = gate_slope_ref.shape[1]
    tile = column_tile(cols)

    def step(j, carry):
        at = pl.ds(pl.multiple_of(j * tile, tile), tile)
        grad = sum(contract_last(g[...], w[at, :]) for g, w in zip(grads, weights))
        gate_ref[:, at] = (grad * gate_slope_ref[:, at].astype(wide)).astype(low)
        up_ref[:, at] = (grad * up_slope_ref[:, at].astype(wide)).astype(low)
        return carry

    lax.fori_loop(0, cols // tile, step, 0)


def units_back(grads, weights, gate_slope, up_slope):
    rows, cols = gate_slope.shape
    tile = next(t for t in (512, 256, 128, rows) if rows % t == 0)
    width = sum(g.shape[1] for g in grads)
    return pl.pallas_call(
        functools.partial(units_back_kernel, len(grads)),
        out_shape=[jax.ShapeDtypeStruct((rows, cols), low)] * 2,
        grid=(rows // tile,),
        in_specs=[pl.BlockSpec((tile, g.shape[1]), lambda i: (i, 0)) for g in grads]
        + [pl.BlockSpec(w.shape, lambda i: (0, 0)) for w in weights]
        + [pl.BlockSpec((tile, cols), lambda i: (i, 0))] * 2,
        out_specs=[pl.BlockSpec((tile, cols), lambda i: (i, 0))] * 2,
        compiler_params=pltpu.CompilerParams(vmem_limit_bytes=56 * 2**20),
        cost_estimate=pl.CostEstimate(
            flops=2 * rows * width * cols,
            bytes_accessed=2 * width * cols + 2 * rows * width + 8 * rows * cols,
            transcendentals=0,
        ),
    )(*grads, *weights, gate_slope, up_slope)


def product_kernel(*refs):
    *lefts, right_ref, out_ref = refs
    depth = lefts[0].shape[1]

    def body(at):
        total = sum(
            contract_last(left[at, :], right_ref[:, i * depth : (i + 1) * depth])
            for i, left in enumerate(lefts)
        )
        out_ref[at, :] = total.astype(out_ref.dtype)

    row_chunks(lefts[0].shape[0], body)


def product_last(lefts, right):
    rows, depth = lefts[0].shape
    cols, width = right.shape
    tile = column_tile(cols)
    return pl.pallas_call(
        product_kernel,
        out_shape=jax.ShapeDtypeStruct((rows, cols), low),
        grid=(cols // tile,),
        in_specs=[pl.BlockSpec((rows, depth), lambda j: (0, 0)) for _ in lefts]
        + [pl.BlockSpec((tile, width), lambda j: (j, 0))],
        out_specs=pl.BlockSpec((rows, tile), lambda j: (0, j)),
        compiler_params=pltpu.CompilerParams(vmem_limit_bytes=48 * 2**20),
        cost_estimate=pl.CostEstimate(
            flops=2 * rows * width * cols,
            bytes_accessed=2 * (rows * width + width * cols + rows * cols),
            transcendentals=0,
        ),
    )(*lefts, right)


def cores_apart_kernel(count, x_ref, out_ref):
    part = x_ref.shape[1] // count
    order = [*range(0, count, 2), *range(1, count, 2)]
    out_ref[...] = jnp.concatenate(
        [x_ref[:, b * part : (b + 1) * part] for b in order], axis=1
    )


def cores_apart(x, count):
    rows, cols = x.shape
    return pl.pallas_call(
        functools.partial(cores_apart_kernel, count),
        out_shape=jax.ShapeDtypeStruct(x.shape, x.dtype),
        grid=(rows // 128,),
        in_specs=[pl.BlockSpec((128, cols), lambda i: (i, 0))],
        out_specs=pl.BlockSpec((128, cols), lambda i: (i, 0)),
        compiler_params=pltpu.CompilerParams(vmem_limit_bytes=32 * 2**20),
        cost_estimate=pl.CostEstimate(
            flops=0, bytes_accessed=4 * rows * cols, transcendentals=0
        ),
    )(x)


def frequencies(half, head_dim):
    return rope_base ** (-(jnp.arange(half, dtype=wide) * 2.0) / head_dim)


def rotate(vectors, cosine, sine):
    half = vectors.shape[-1] // 2
    first = vectors[..., :half]
    second = vectors[..., half:]
    return jnp.concatenate(
        [first * cosine - second * sine, second * cosine + first * sine], axis=-1
    )


def inverse_rms(vectors):
    return lax.rsqrt(jnp.mean(vectors * vectors, axis=-1, keepdims=True) + epsilon)


def norm_back(vectors, inverse, gain, upstream):
    scaled = upstream * gain
    unit = vectors * inverse
    grad_vectors = inverse * (scaled - unit * jnp.mean(unit * scaled, axis=-1, keepdims=True))
    return (grad_vectors, jnp.sum(upstream * unit, axis=0))


def dot(left, right):
    return jnp.dot(left, right, preferred_element_type=wide)


def contract_last(left, right):
    return lax.dot_general(left, right, (((1,), (1,)), ((), ())), preferred_element_type=wide)


def contract_first(left, right):
    return lax.dot_general(left, right, (((0,), (0,)), ((), ())), preferred_element_type=wide)


def per_device(
    inputs,
    positions,
    pre_attn_gain,
    post_attn_gain,
    pre_mlp_gain,
    post_mlp_gain,
    query_weight,
    key_weight,
    value_weight,
    out_weight,
    gate_weight,
    up_weight,
    down_weight,
    cotangent,
):
    n_ctx, n_fsdp = lax.axis_size("ctx"), lax.axis_size("fsdp")
    c, f = lax.axis_index("ctx"), lax.axis_index("fsdp")
    rows = inputs[0].astype(wide)
    tokens, width = rows.shape
    length = n_ctx * tokens
    scale = HD ** (-0.5)
    my_heads = HQ // n_ctx
    my_kv = max(KV // n_ctx, 1)
    share = max(n_ctx // KV, 1)
    groups = my_heads // my_kv
    kv_start = (c // share) * my_kv * HD
    query_cols, kv_cols = my_heads * HD, my_kv * HD
    out_cols = width // n_ctx
    ff_rows = down_weight.shape[0]
    part = ff_rows // n_ctx
    main = ff_rows // 128 // n_ctx * 128
    rest = part - main
    chips = n_fsdp // 2
    tiled = ff_rows % 128 == 0 and main > 0 and rest * n_ctx == 128 and rest % 16 == 0
    tiled = tiled and chips * rest % 128 == 0 and query_cols % 256 == 0
    last_cols = width // 384 * 128

    def gathered(shard):
        return lax.all_gather(shard, "fsdp", axis=0, tiled=True)

    def units_together(full):
        if not tiled:
            return full
        moves = []
        for block in range(n_fsdp):
            to = unit_place(block, n_fsdp, main, rest)
            moves.append((block * part, main, to, 0))
            to = rest_place(block % 2, n_fsdp, main, rest) + block // 2 * rest
            moves.append((block * part + main, rest, to, 0))
        return place([(full, 0, moves)], jnp.zeros((), jnp.int32), full.shape, 0, full.dtype)

    def chip_term(term):
        return chip_sum(term.astype(low))

    def unit_term(left, right):
        if not tiled:
            return chip_term(contract_first(left, right))
        half, core = chips * part, f & 1
        theirs = lax.dynamic_slice_in_dim(left, (1 - core) * half, half, 1)
        theirs = swap(contract_first(theirs, right).astype(low), "fsdp", 1)
        mine = contract_first(lax.dynamic_slice_in_dim(left, core * half, half, 1), right)
        moves = [(chip * main, main, chip * part) for chip in range(chips)]
        moves += [
            (chips * main + chip * rest, rest, chip * part + main) for chip in range(chips)
        ]
        return add_rows(mine.astype(low), theirs, moves)

    def weight_term(left, right):
        if not tiled:
            return chip_term(contract_first(left, right))
        half, core = left.shape[1] // 2, f & 1
        theirs = lax.dynamic_slice_in_dim(left, (1 - core) * half, half, 1)
        theirs = swap(contract_first(theirs, right).astype(low), "fsdp", 1)
        mine = contract_first(lax.dynamic_slice_in_dim(left, core * half, half, 1), right)
        return (mine + theirs.astype(wide)).astype(low)

    def my_units(weight):
        if tiled:
            return take_units(weight, c, n_fsdp, main, rest)
        split = weight.reshape(weight.shape[0], n_fsdp, n_ctx, part)
        return lax.dynamic_index_in_dim(split, c, 2, keepdims=False).reshape(
            weight.shape[0], n_fsdp * part
        )

    def in_order(blocks):
        blocks = list(blocks)
        for bit in range(n_ctx.bit_length() - 1):
            mask = 1 << bit
            odd = (c & mask) != 0
            blocks = [jnp.where(odd, blocks[k ^ mask], blocks[k]) for k in range(n_ctx)]
        return blocks

    def token_blocks(array):
        return [array[k * tokens : (k + 1) * tokens] for k in range(n_ctx)]

    def block_order(blocks, k):
        pieces = blocks.reshape(n_ctx, tokens, blocks.shape[-1])
        return jnp.concatenate([pieces[k ^ m] for m in range(n_ctx)], axis=0)

    def from_columns(array):
        got = jnp.stack(exchange(token_blocks(array)))
        return jnp.transpose(jnp.take(got, jnp.arange(n_ctx) ^ c, axis=0), (1, 0, 2)).reshape(
            tokens, width
        )

    def to_columns(array):
        split = array.reshape(tokens, n_ctx, out_cols)
        split = jnp.take(split, jnp.arange(n_ctx) ^ c, axis=1)
        return jnp.concatenate(exchange([split[:, k] for k in range(n_ctx)]), axis=0)

    my_qkv = jnp.concatenate(
        [
            lax.dynamic_slice_in_dim(query_weight, c * query_cols, query_cols, 1),
            lax.dynamic_slice_in_dim(key_weight, kv_start, kv_cols, 1),
            lax.dynamic_slice_in_dim(value_weight, kv_start, kv_cols, 1),
        ],
        axis=1,
    )
    full_qkv = gathered(my_qkv)
    full_out = gathered(lax.dynamic_slice_in_dim(out_weight, c * out_cols, out_cols, 1))
    full_units = gathered(jnp.concatenate([my_units(gate_weight), my_units(up_weight)], axis=1))
    if tiled:
        my_down = jnp.concatenate(
            [
                lax.dynamic_slice_in_dim(down_weight, c * main, main, 0),
                lax.dynamic_slice_in_dim(down_weight, n_ctx * main + c * rest, rest, 0),
            ],
            axis=0,
        )
    else:
        my_down = lax.dynamic_slice_in_dim(down_weight, c * part, part, 0)
    gains = jnp.stack([pre_attn_gain, post_attn_gain, pre_mlp_gain, post_mlp_gain])
    gains = jnp.stack([gains if k == 0 else swap(gains, "fsdp", k) for k in range(n_fsdp)])
    gains = jnp.take(gains, jnp.arange(n_fsdp) ^ f, axis=0)
    gains = jnp.transpose(gains, (1, 0, 2)).reshape(4, width).astype(wide)
    gain_a, gain_b, gain_c, gain_d = gains[0], gains[1], gains[2], gains[3]

    inverse_a = inverse_rms(rows)
    normed = join(gather_pieces((rows * inverse_a * gain_a).astype(low)))
    places = jnp.concatenate(gather_blocks(positions[0], halves=False), axis=0)
    angles = places.astype(wide)[:, None] * frequencies(HD // 2, HD)
    cosine, sine = jnp.cos(angles), jnp.sin(angles)
    projected = dot(normed, full_qkv)
    query_lin = projected[:, :query_cols].reshape(length, my_heads, HD)
    key_lin = projected[:, query_cols : query_cols + kv_cols].reshape(length, my_kv, HD)
    values = projected[:, query_cols + kv_cols :].astype(low).reshape(length, my_kv, HD)
    queries = (rotate(query_lin, cosine[:, None], sine[:, None]) * scale).astype(low)
    keys = rotate(key_lin, cosine[:, None], sine[:, None]).astype(low)
    queries = queries.reshape(length, my_kv, groups, HD)
    allowed = places[None, :] <= places[:, None]
    raw = jnp.einsum("tkgd,rkd->kgtr", queries, keys, preferred_element_type=wide)
    bent = jnp.tanh(raw / soft_cap)
    weights = jnp.where(allowed, jnp.exp(soft_cap * bent), 0.0)
    total = jnp.sum(weights, axis=-1)
    mixed = jnp.einsum("kgtr,rkd->kgtd", weights.astype(low), values, preferred_element_type=wide)
    mixed = mixed / total[..., None]
    attn = jnp.transpose(mixed, (2, 0, 1, 3)).reshape(length, query_cols).astype(low)

    if tiled:
        pieces = [
            (array, k, [(0, array.shape[1], first, query_cols)])
            for array, k, first in gather_pieces(attn)
        ]
        attn_all = place(pieces, c, (length, HQ * HD), 1, low, blocks=n_ctx)
    else:
        attn_blocks = [block_order(block, k) for k, block in enumerate(gather_blocks(attn))]
        attn_all = jnp.concatenate(in_order(attn_blocks), axis=1)
    branch = from_columns(dot(attn_all, full_out).astype(low)).astype(wide)
    inverse_b = inverse_rms(branch)
    middle = rows + branch * inverse_b * gain_b
    inverse_c = inverse_rms(middle)

    normed_mlp = join(gather_pieces((middle * inverse_c * gain_c).astype(low)))
    normed_mlp_apart = cores_apart(normed_mlp, n_fsdp) if tiled else normed_mlp
    my_down = after(my_down, full_units, normed_mlp_apart)
    first_down, last_down = gathered(my_down[:, :-last_cols]), my_down[:, -last_cols:]
    hidden, gate_slope, up_slope = units_forward(normed_mlp, full_units)
    last_down = gathered(after(last_down, first_down, hidden))
    full_downs = [units_together(first_down), units_together(last_down)]
    first_terms, last_terms = (
        token_blocks(dot(hidden, full).astype(low)) for full in full_downs
    )
    last_terms = sum(term.astype(wide) for term in exchange(last_terms))
    down = jnp.concatenate([scatter_sum(halved(first_terms)), last_terms], axis=1)
    inverse_d = inverse_rms(down)
    output = (middle + down * inverse_d * gain_d).astype(low)[None]

    grad_result = cotangent[0].astype(wide)
    grad_down, grad_gain_d = norm_back(down, inverse_d, gain_d, grad_result)
    grad_down = grad_down.astype(low)
    pieces = gather_pieces(grad_down[:, -last_cols:])
    grad_downs = [join(pieces)]
    down_terms = [unit_term(hidden, grad_downs[0])]
    others = [array for array, _, _ in pieces[1:3]]
    pieces = gather_pieces(after(grad_down[:, :-last_cols], *others))
    pieces[0] = (after(pieces[0][0], down_terms[0]), *pieces[0][1:])
    grad_downs.append(join(pieces))
    down_terms.append(unit_term(hidden, grad_downs[1]))
    grad_downs, down_terms[1] = lax.optimization_barrier((grad_downs, down_terms[1]))
    down_sums = [fsdp_sum(term) for term in down_terms]
    grad_gate, grad_up = units_back(grad_downs, full_downs[::-1], gate_slope, up_slope)
    grad_normed_mlp = product_last([grad_gate, grad_up], full_units)
    grad_normed_mlp, grad_gate = lax.optimization_barrier((grad_normed_mlp, grad_gate))
    gate_term = weight_term(normed_mlp_apart, after(grad_gate, down_sums[0]))
    gate_sum = fsdp_sum(gate_term)
    up_term = weight_term(normed_mlp_apart, after(grad_up, gate_term))
    up_sum = fsdp_sum(up_term)
    grad_normed_mlp = scatter_sum(halved(token_blocks(grad_normed_mlp)))
    down_pieces = [gather_pieces(after(down_sums[0], grad_gate))]
    arrived = [piece[0] for piece in down_pieces[0]]
    grad_normed_mlp = after(grad_normed_mlp, up_term, down_sums[1], *arrived)
    down_pieces.append(gather_pieces(after(down_sums[1], grad_normed_mlp)))
    grad_middle_mlp, grad_gain_c = norm_back(middle, inverse_c, gain_c, grad_normed_mlp)
    grad_middle = grad_result + grad_middle_mlp
    grad_branch, grad_gain_b = norm_back(branch, inverse_b, gain_b, grad_middle)

    arrived = [piece[0] for piece in down_pieces[1][1:3]]
    grad_branch_cols = to_columns(after(grad_branch.astype(low), *arrived))
    out_term = contract_first(attn_all, grad_branch_cols).astype(low)
    grad_attn_all = contract_last(grad_branch_cols, full_out).astype(low)
    if tiled:
        parts = split_columns(grad_attn_all, c, n_ctx, cut_at(query_cols))
        grad_attn = scatter_sum(list(zip(parts[::2], parts[1::2]))).astype(low)
    else:
        parts = [
            lax.dynamic_slice_in_dim(grad_attn_all, (c ^ k) * query_cols, query_cols, 1)
            for k in range(n_ctx)
        ]
        parts = [block_order(part_, k) for k, part_ in enumerate(parts)]
        grad_attn = scatter_sum(halved(parts)).astype(low)
    grad_attn = after(grad_attn, gate_sum, *[piece[0] for piece in down_pieces[1]])
    gate_pieces = gather_pieces(after(gate_sum, grad_attn))
    grad_projected = attention_back(
        grad_attn,
        queries.reshape(length, query_cols),
        keys.reshape(length, kv_cols),
        values.reshape(length, kv_cols),
        places,
        cosine,
        sine,
        scale,
    )
    grad_projected = after(grad_projected, *[piece[0] for piece in gate_pieces[1:3]])
    qkv_term = contract_first(normed, grad_projected).astype(low)
    pad = (qkv_term.shape[0] - out_term.shape[0]) // n_fsdp
    out_term = jnp.pad(out_term.reshape(n_fsdp, -1, out_cols), ((0, 0), (0, pad), (0, 0)))
    out_term = out_term.reshape(qkv_term.shape[0], out_cols)
    attn_sum = lax.psum_scatter(
        jnp.concatenate([qkv_term, out_term], axis=1), "fsdp", scatter_dimension=0, tiled=True
    )
    qkv_sum = attn_sum[:, : qkv_term.shape[1]]
    out_sum = attn_sum[: attn_sum.shape[0] - pad, qkv_term.shape[1] :]
    grad_normed = contract_last(grad_projected, full_qkv).astype(low)
    grad_normed = scatter_sum(halved(token_blocks(grad_normed)))
    grad_normed = after(grad_normed, up_sum)
    grad_rows, grad_gain_a = norm_back(rows, inverse_a, gain_a, grad_normed)
    input_grad = (grad_middle + grad_rows).astype(low)[None]

    gain_terms = jnp.stack([grad_gain_a, grad_gain_b, grad_gain_c, grad_gain_d])
    gain_terms = jnp.transpose(gain_terms.reshape(4, n_fsdp, width // n_fsdp), (1, 0, 2))
    gain_terms = jnp.take(gain_terms, jnp.arange(n_fsdp) ^ f, axis=0)
    gain_sums = gain_terms[0]
    for k in range(1, n_fsdp):
        gain_sums = gain_sums + swap(gain_terms[k], "fsdp", k)
    gain_sums = sum(in_order(exchange([gain_sums] * n_ctx)))

    if share == 1:
        qkv_pieces = gather_pieces(qkv_sum)

        def columns_of(first, size, shape):
            pieces = []
            for array, k, start in qkv_pieces:
                begin, end = max(first, start), min(first + size, start + array.shape[1])
                if begin < end:
                    pieces.append((array, k, [(begin - start, size, 0, size)]))
            return place(pieces, c, shape, 1, wide)

        query_grad = columns_of(0, query_cols, query_weight.shape)
        key_grad = columns_of(query_cols, kv_cols, key_weight.shape)
        value_grad = columns_of(query_cols + kv_cols, kv_cols, value_weight.shape)
    else:
        qkv_blocks = gather_blocks(qkv_sum)
        query_grad = jnp.zeros(query_weight.shape, wide)
        key_grad = jnp.zeros(key_weight.shape, wide)
        value_grad = jnp.zeros(value_weight.shape, wide)
        for k, block in enumerate(qkv_blocks):
            query_grad = lax.dynamic_update_slice_in_dim(
                query_grad, block[:, :query_cols].astype(wide), (c ^ k) * query_cols, 1
            )
        for k in range(0, n_ctx, share):
            block = sum(qkv_blocks[k + s][:, query_cols:].astype(wide) for s in range(share))
            start = ((c ^ k) // share) * kv_cols
            key_grad = lax.dynamic_update_slice_in_dim(key_grad, block[:, :kv_cols], start, 1)
            value_grad = lax.dynamic_update_slice_in_dim(value_grad, block[:, kv_cols:], start, 1)

    out_grad = jnp.concatenate(in_order(gather_blocks(out_sum)), axis=1).astype(wide)

    def all_units(gathered_pieces):
        if not tiled:
            blocks = as_blocks(gathered_pieces)
            blocks = [b.reshape(b.shape[0], n_fsdp, part) for b in in_order(blocks)]
            return jnp.stack(blocks, axis=2).reshape(gate_weight.shape).astype(wide)
        pieces, tails = [], []
        for array, k, start in gathered_pieces:
            moves = []
            for b in range(n_fsdp):
                begin = unit_place(b, n_fsdp, main, rest) - start
                if 0 <= begin < array.shape[1]:
                    moves.append((begin, main, b * ff_rows, main))
            pieces.append((array, k, moves))
            for core in (0, 1):
                begin = rest_place(core, n_fsdp, main, rest) - start
                if 0 <= begin < array.shape[1]:
                    tails.append((k, core, array[:, begin : begin + chips * rest]))
        tails = [tail for _, _, tail in sorted(tails, key=lambda item: item[:2])]
        source = jnp.arange(n_ctx * n_fsdp * rest)[:, None]
        index, unit = source // (n_fsdp * rest), source % (n_fsdp * rest)
        block = unit // rest % chips * 2 + unit // (chips * rest)
        target = block * 128 + (c ^ index) * rest + unit % rest
        spread_to = (target == jnp.arange(n_fsdp * 128)[None, :]).astype(low)
        return place(
            pieces,
            c,
            gate_weight.shape,
            1,
            wide,
            dot(jnp.concatenate(tails, axis=1), spread_to),
            [(b * 128, 128, (b + 1) * ff_rows - 128) for b in range(n_fsdp)],
        )

    gate_arrays = lax.optimization_barrier(([piece[0] for piece in gate_pieces], qkv_term))[0]
    gate_grad = all_units([(a, *piece[1:]) for a, piece in zip(gate_arrays, gate_pieces)])
    up_grad = all_units(gather_pieces(up_sum))
    down_halves = zip(*[as_blocks(pieces) for pieces in down_pieces[::-1]])
    down_blocks = [jnp.concatenate(block, axis=1) for block in down_halves]
    down_blocks[0] = after(down_blocks[0], qkv_term)
    if tiled:
        moves = [(0, main, 0, main), (main, rest, n_ctx * main, rest)]
        pieces = [(block, k, moves) for k, block in enumerate(down_blocks)]
        down_grad = place(pieces, c, down_weight.shape, 0, wide)
    else:
        down_grad = jnp.concatenate(in_order(down_blocks), axis=0).astype(wide)
    return (
        output,
        input_grad,
        gain_sums[0],
        gain_sums[1],
        gain_sums[2],
        gain_sums[3],
        query_grad,
        key_grad,
        value_grad,
        out_grad,
        gate_grad,
        up_grad,
        down_grad,
    )


def solution(mesh):
    return jax.shard_map(
        per_device,
        mesh=mesh,
        in_specs=(
            P("fsdp", "ctx", None),
            P("fsdp", "ctx"),
            P("fsdp"),
            P("fsdp"),
            P("fsdp"),
            P("fsdp"),
            P("fsdp", None),
            P("fsdp", None),
            P("fsdp", None),
            P("fsdp", None),
            P("fsdp", None),
            P("fsdp", None),
            P("fsdp", None),
            P("fsdp", "ctx", None),
        ),
        out_specs=(
            P("fsdp", "ctx", None),
            P("fsdp", "ctx", None),
            P("fsdp"),
            P("fsdp"),
            P("fsdp"),
            P("fsdp"),
            P("fsdp", None),
            P("fsdp", None),
            P("fsdp", None),
            P("fsdp", None),
            P("fsdp", None),
            P("fsdp", None),
            P("fsdp", None),
        ),
        check_vma=False,
    )
```
